32 devices in a mesh: gx: 4 (over y, x), gy: 2 (over core), gz: 4 (over z).
Axes of the slice: x: 2, y: 2, z: 4, core: 2. Of those that a mesh axis runs over, the one named last changes fastest.
Arguments:
- offsets: float32 [4, 2, 4, 3, 128], P('gx', 'gy', 'gz'), may hold values from 0 to 10
- features: bfloat16 [4, 2, 4, 128, 256], P('gx', 'gy', 'gz'), may hold values from -6 to 6
- counts: int32 [4, 2, 4], P('gx', 'gy', 'gz'), may hold values from 64 to 128
- mask: int32 [4, 2, 4, 128], P('gx', 'gy', 'gz'), may hold values 0 or 1
- targets: float32 [4, 2, 4, 3, 128], P('gx', 'gy', 'gz'), may hold values from -6 to 6
- w_in: bfloat16 [256, 256], replicated, may hold values from -0.375 to 0.375
- radial: float32 [6, 256], replicated, may hold values from -5 to 5
- readout: float32 [256], replicated, may hold values from -0.375 to 0.375
Outputs:
- prediction: float32 [4, 2, 4, 3, 128], P('gx', 'gy', 'gz')
- grad_features: float32 [4, 2, 4, 128, 256], P('gx', 'gy', 'gz')
The draws below stay inside these ranges and needn't reach their ends.
All inputs are finite; a program needn't handle non-finite values. No bound on the sum of `mask` on one device may be relied on, other than what follows from the above.
Results may differ from the reference program's by a relative error of at most 0.0065.
Values may be sent and summed in bfloat16 or wider, within the bound.
No kernel may reach another device: no remote copies, remote signals or barrier semaphores. Data moves between devices by JAX's collectives and lax.ppermute only.
A program may use at most 64 MiB of HBM per device.

```python
import jax
import jax.numpy as jnp
from jax import lax

F = 256
NB = 6
ATOM_DEV = 128
N_GX = 4
N_GY = 2
N_GZ = 4


def plant(entries, rng, least, top_value):
    longest = entries.shape.index(max(entries.shape))
    spots = []
    for shift in (0, 1):
        where = [jax.random.randint(jax.random.fold_in(rng, axis), (), 0, length) for axis, length in enumerate(entries.shape)]
        where[longest] = (where[longest] + shift) % entries.shape[longest]
        spots.append(tuple(where))
    return entries.at[spots[0]].set(least).at[spots[1]].set(top_value)


def level_of(key, shape, split, low, largest):
    def one(dim, parts):
        draws = jax.random.uniform(jax.random.fold_in(jax.random.fold_in(key, 6), dim), (parts,), jnp.float32, low / len(split), largest / len(split))
        return jnp.repeat(jnp.exp(draws), shape[dim] // parts).reshape((-1,) + (1,) * (len(shape) - dim - 1))

    gain = one(*split[0])
    for cut in split[1:]:
        gain = gain * one(*cut)
    return gain


def centred(stream_key, extent, deviation, bound, shards=(), kind=jnp.bfloat16):
    factor_of = level_of(stream_key, extent, shards, -0.22, 0.18) if shards else 1.0
    values = jax.random.normal(stream_key, extent, jnp.float32) * deviation * factor_of
    return jnp.minimum(jnp.maximum(values, -bound), bound).astype(kind)


def setup_inputs(seed: int = 0) -> dict:
    key_of = jax.random.split(jax.random.key(seed), 9)
    return {
        "offsets": jnp.clip(10.0 * jax.random.uniform(key_of[0], (N_GX, N_GY, N_GZ, 3, ATOM_DEV), jnp.float32) ** level_of(key_of[0], (N_GX, N_GY, N_GZ, 3, ATOM_DEV), ((0, 4), (1, 2), (2, 4)), -0.2, 0.2), 0.0, 10.0),
        "features": centred(key_of[1], (N_GX, N_GY, N_GZ, ATOM_DEV, F), 1.0, 6.0, ((0, 4), (1, 2), (2, 4))),
        "counts": plant(jax.random.randint(key_of[2], (N_GX, N_GY, N_GZ), ATOM_DEV // 2, ATOM_DEV + 1), jax.random.fold_in(key_of[2], 1), ATOM_DEV // 2, ATOM_DEV).astype(jnp.int32),
        "mask": plant((jax.random.randint(key_of[3], (N_GX, N_GY, N_GZ, ATOM_DEV), 0, 2) < 1).astype(jnp.int32), jax.random.fold_in(key_of[3], 1), 0, 1),
        "targets": centred(key_of[4], (N_GX, N_GY, N_GZ, 3, ATOM_DEV), 1.0, 6.0, ((0, 4), (1, 2), (2, 4)), jnp.float32),
        "w_in": centred(key_of[5], (F, F), F ** -0.5, 0.375),
        "radial": centred(key_of[6], (NB, F), 1.0, 5.0, (), jnp.float32),
        "readout": centred(key_of[7], (F,), F ** -0.5, 0.375, (), jnp.float32),
    }


EDGE = 10.0
CUT = 5.0
GAMMA = 20.0
LOSS_WEIGHT = 16.0


def slot_shift(first, count):
    slot = first + jnp.arange(count, dtype=jnp.int32)
    step_x = slot // 9 - 1
    step_y = (slot // 3) % 3 - 1
    step_z = slot % 3 - 1
    return jnp.stack([step_x, step_y, step_z], 1).astype(jnp.float32) * EDGE


def build_kernels(own, near, first, count, bases):
    atoms = own.shape[1]
    shift = slot_shift(first, count)
    placed = near[:, :3, :] + shift[:, :, None]
    placed = jnp.transpose(placed, (1, 0, 2)).reshape(3, count * atoms)
    weight_near = near[:, 3, :].reshape(count * atoms)
    apart = placed[:, None, :] - own[:3, :, None]
    ratio = (apart[0] * apart[0] + apart[1] * apart[1] + apart[2] * apart[2]) / (CUT * CUT)
    column = first * atoms + jnp.arange(count * atoms, dtype=jnp.int32)
    same = column[None, :] == (13 * atoms + jnp.arange(atoms, dtype=jnp.int32))[:, None]
    envelope = jnp.where(same, 0.0, jnp.square(jnp.maximum(1.0 - ratio, 0.0)))
    envelope = envelope * own[3][:, None] * weight_near[None, :]
    centers = jnp.arange(bases).astype(jnp.float32) / (bases - 1)
    radial_part = envelope[None] * jnp.exp(-GAMMA * jnp.square(ratio[None] - centers[:, None, None]))
    direction_part = envelope[None] * apart / CUT
    return jnp.concatenate([radial_part, direction_part], 0).astype(jnp.bfloat16)


def neighbours(grid, index):
    plane = N_GY * N_GZ
    pos_x = index // plane
    pos_y = (index // N_GZ) % N_GY
    pos_z = index % N_GZ
    slot = jnp.arange(27, dtype=jnp.int32)
    near_x = (pos_x + slot // 9 - 1) % N_GX
    near_y = (pos_y + (slot // 3) % 3 - 1) % N_GY
    near_z = (pos_z + slot % 3 - 1) % N_GZ
    return grid[near_x, near_y, near_z]


def reference(offsets, features, counts, mask, targets, w_in, radial, readout):
    bases = radial.shape[0]
    atoms = features.shape[3]
    width = features.shape[4]
    occ = (jnp.arange(atoms, dtype=jnp.int32)[None, None, None, :] < counts[..., None]).astype(jnp.float32)
    coords = jnp.concatenate([offsets, occ[:, :, :, None, :]], 3)
    proj = jnp.dot(features.reshape(-1, width), w_in, preferred_element_type=jnp.float32)
    proj = proj.astype(jnp.bfloat16).reshape(features.shape)
    flat_coords = coords.reshape(-1, 4, atoms)
    flat_mask = mask.reshape(-1, atoms).astype(jnp.float32)
    flat_targets = targets.reshape(-1, 3, atoms)
    hp = lax.Precision.HIGHEST
    count_all = N_GX * N_GY * N_GZ

    def forward_one(index):
        own = flat_coords[index]
        kern = build_kernels(own, neighbours(coords, index), 0, 27, bases)
        near_proj = neighbours(proj, index).reshape(27 * atoms, width)
        msg = jnp.einsum('kij,jf->kif', kern.astype(jnp.float32), near_proj.astype(jnp.float32))
        pre = jnp.einsum('bf,bif->if', radial, msg[:bases], precision=hp)
        gate = jax.nn.sigmoid(pre)
        gates = readout[None, :] * gate
        vec = msg[bases:]
        pred = jnp.einsum('cif,if->ci', vec, gates, precision=hp)
        err = LOSS_WEIGHT * flat_mask[index][None, :] * own[3][None, :] * (pred - flat_targets[index])
        slope = jnp.einsum('ci,cif->if', err, vec, precision=hp) * readout[None, :] * gate * (1.0 - gate)
        return pred, err, slope.astype(jnp.bfloat16), gates.astype(jnp.bfloat16)

    pred, err, slope, gates_bf = lax.map(forward_one, jnp.arange(count_all, dtype=jnp.int32))
    err_grid = err.reshape(N_GX, N_GY, N_GZ, 3, atoms)
    slope_grid = slope.reshape(N_GX, N_GY, N_GZ, atoms, width)
    gates_grid = gates_bf.reshape(N_GX, N_GY, N_GZ, atoms, width)

    def backward_one(index):
        own = flat_coords[index]
        kern = build_kernels(own, neighbours(coords, index), 0, 27, bases)
        near_err = jnp.transpose(neighbours(err_grid, index), (1, 0, 2)).reshape(3, 27 * atoms)
        near_slope = neighbours(slope_grid, index).reshape(27 * atoms, width)
        near_gates = neighbours(gates_grid, index).reshape(27 * atoms, width)
        wide = kern[bases:].astype(jnp.float32)
        pairs = wide[0] * near_err[0][None, :] + wide[1] * near_err[1][None, :] + wide[2] * near_err[2][None, :]
        pairs = pairs.astype(jnp.bfloat16)
        radial_sum = jnp.einsum('bij,jf->bif', kern[:bases].astype(jnp.float32), near_slope.astype(jnp.float32))
        cross = jnp.dot(pairs, near_gates, preferred_element_type=jnp.float32)
        back = jnp.einsum('bf,bif->if', radial, radial_sum, precision=hp) - cross
        return jnp.dot(back.astype(jnp.bfloat16), w_in.T, preferred_element_type=jnp.float32)

    grad = lax.map(backward_one, jnp.arange(count_all, dtype=jnp.int32))
    prediction = pred.reshape(N_GX, N_GY, N_GZ, 3, atoms)
    return prediction, grad.reshape(N_GX, N_GY, N_GZ, atoms, width)
```

```python
import functools
import itertools
import math

import jax
import jax.numpy as jnp
from jax import lax
from jax.experimental import pallas as pl
from jax.experimental.pallas import tpu as pltpu
from jax.sharding import PartitionSpec as P

EDGE = 10.0
CUT = 5.0
GAMMA = 20.0
LOSS_WEIGHT = 16.0
FAR = 1000.0
TAIL = 16


def steps_of(size):
    return (0, None) if size == 2 else (0, -1, 1)


def shift(block, axis, step):
    size = lax.axis_size(axis)
    return lax.ppermute(block, axis, [(i, (i + step) % size) for i in range(size)])


def spread(blocks, axis):
    parts = [blocks]
    for step in steps_of(lax.axis_size(axis))[1:]:
        parts.append(shift(blocks, axis, 1 if step is None else -step))
    return parts


def collect(blocks, axis):
    total = blocks[0]
    for part, step in zip(blocks[1:], steps_of(lax.axis_size(axis))[1:]):
        total = total + shift(part, axis, 1 if step is None else step)
    return total


def message_kernel(feat_ref, w_ref, offs_ref, occ_ref, out_ref):
    atoms, width = feat_ref.shape
    out_ref[:atoms, :] = jnp.dot(
        feat_ref[...], w_ref[...], preferred_element_type=jnp.float32
    ).astype(jnp.bfloat16)
    place = jnp.where(occ_ref[...] > 0.0, offs_ref[...], -FAR)
    high = place.astype(jnp.bfloat16)
    rest = place - high.astype(jnp.float32)
    middle = rest.astype(jnp.bfloat16)
    low = (rest - middle.astype(jnp.float32)).astype(jnp.bfloat16)
    rows = jnp.concatenate(
        [
            high.astype(jnp.float32),
            middle.astype(jnp.float32),
            low.astype(jnp.float32),
            jnp.zeros((TAIL - 9, atoms), jnp.float32),
        ],
        0,
    )
    out_ref[atoms:, :atoms] = rows.astype(jnp.bfloat16)
    if width > atoms:
        out_ref[atoms:, atoms:] = jnp.zeros((TAIL, width - atoms), jnp.bfloat16)


def across(row, count):
    return jnp.transpose(jnp.broadcast_to(row, (count, row.shape[1])))


def pair_kernel(
    slots, bases, offs_ref, occ_ref, mask_ref, targ_ref, radial_ref, readout_ref, *refs
):
    groups = len(refs) - 5
    near_refs, (pred_ref, mine_ref, theirs_ref, kern_ref, proj_ref) = refs[:groups], refs[groups:]
    atoms = offs_ref.shape[1]
    width = radial_ref.shape[1]
    columns = near_refs[0].shape[0]
    rate = 2.0 * GAMMA / (bases - 1)
    occ = occ_ref[...]
    own = [across(jnp.where(occ > 0.0, offs_ref[c : c + 1, :], FAR), atoms) for c in range(3)]
    for s, steps in enumerate(slots):
        group, place = divmod(s, columns)
        block = near_refs[group].at[place]
        proj_ref[s * atoms : (s + 1) * atoms, :] = block[:atoms, :]
        coded = block[atoms:, :atoms].astype(jnp.float32)
        apart = []
        for c in range(3):
            spot = coded[c : c + 1, :] + coded[3 + c : 4 + c, :] + coded[6 + c : 7 + c, :]
            if steps[c] is None:
                away = spot - own[c]
                apart.append(away + jnp.where(away < 0.0, EDGE, -EDGE))
            elif steps[c] == 0:
                apart.append(spot - own[c])
            else:
                apart.append((spot + steps[c] * EDGE) - own[c])
        ratio = (apart[0] * apart[0] + apart[1] * apart[1] + apart[2] * apart[2]) * (
            1.0 / (CUT * CUT)
        )
        ratio = jnp.minimum(ratio, 1.0)
        if steps == (0, 0, 0):
            same = lax.broadcasted_iota(jnp.int32, (atoms, atoms), 0) == lax.broadcasted_iota(
                jnp.int32, (atoms, atoms), 1
            )
            ratio = jnp.where(same, 1.0, ratio)
        envelope = jnp.square(1.0 - ratio)
        value = envelope * jnp.exp(-GAMMA * jnp.square(ratio))
        growth = jnp.exp(rate * ratio)
        lanes = slice(s * atoms, (s + 1) * atoms)
        for b in range(bases):
            kern_ref[b * atoms : (b + 1) * atoms, lanes] = value.astype(jnp.bfloat16)
            if b + 1 < bases:
                value = value * growth
        envelope = envelope * (1.0 / CUT)
        for c in range(3):
            kern_ref[(bases + c) * atoms : (bases + c + 1) * atoms, lanes] = (
                envelope * apart[c]
            ).astype(jnp.bfloat16)

    msg = jnp.dot(kern_ref[...], proj_ref[...], preferred_element_type=jnp.float32)
    fold = [math.exp(-GAMMA * (b / (bases - 1)) ** 2) for b in range(bases)]
    weight = [radial_ref[b : b + 1, :] * fold[b] for b in range(bases)]
    pre = weight[0] * msg[:atoms]
    for b in range(1, bases):
        pre = pre + weight[b] * msg[b * atoms : (b + 1) * atoms]
    gate = 1.0 / (1.0 + jnp.exp(-pre))
    readout = readout_ref[...]
    gates = readout * gate
    vec = [msg[(bases + c) * atoms : (bases + c + 1) * atoms] for c in range(3)]
    lean = jnp.zeros((atoms, width), jnp.float32)
    sides = []
    for c in range(3):
        pred = jnp.sum(gates * vec[c], axis=1, keepdims=True)
        pred = jnp.transpose(jnp.broadcast_to(pred, (atoms, atoms)))[0:1, :]
        pred_ref[c : c + 1, :] = pred
        err = LOSS_WEIGHT * mask_ref[...] * occ * (pred - targ_ref[c : c + 1, :])
        err = across(err, width)
        lean = lean + err * vec[c]
        sides.append((err * gates).astype(jnp.bfloat16))
    slope = lean * readout * gate * (1.0 - gate)
    right = jnp.concatenate([(weight[b] * slope).astype(jnp.bfloat16) for b in range(bases)] + sides, 0)
    for s, steps in enumerate(slots):
        lanes = slice(s * atoms, (s + 1) * atoms)
        back = lax.dot_general(
            right, kern_ref[:, lanes], (((0,), (0,)), ((), ())), preferred_element_type=jnp.float32
        ).astype(jnp.bfloat16)
        group, place = divmod(s, columns)
        if group == 0:
            mine_ref[place] = back
        else:
            theirs_ref[group - 1, place] = back


def on_device(offsets, features, counts, mask, targets, w_in, radial, readout):
    atoms = features.shape[3]
    width = features.shape[4]
    bases = radial.shape[0]
    offs = offsets[0, 0, 0]
    occ = (jnp.arange(atoms, dtype=jnp.int32) < counts[0, 0, 0]).astype(jnp.float32)[None, :]
    vmem = pl.BlockSpec(memory_space=pltpu.VMEM)
    message = pl.pallas_call(
        message_kernel,
        out_shape=jax.ShapeDtypeStruct((atoms + TAIL, width), jnp.bfloat16),
        in_specs=[vmem] * 4,
        out_specs=vmem,
        name="message",
    )(features[0, 0, 0], w_in, offs, occ)

    steps_x, steps_y, steps_z = (steps_of(lax.axis_size(a)) for a in ("gx", "gy", "gz"))
    near = message[None]
    near = jnp.concatenate(spread(near, "gz"), 0)
    near = jnp.concatenate(spread(near, "gx"), 0)
    near = spread(near, "gy")
    columns = len(steps_x) * len(steps_z)
    slots = [(x, y, z) for y, x, z in itertools.product(steps_y, steps_x, steps_z)]

    pred, mine, theirs = pl.pallas_call(
        functools.partial(pair_kernel, slots, bases),
        out_shape=(
            jax.ShapeDtypeStruct((3, atoms), jnp.float32),
            jax.ShapeDtypeStruct((columns, width, atoms), jnp.bfloat16),
            jax.ShapeDtypeStruct((len(steps_y) - 1, columns, width, atoms), jnp.bfloat16),
        ),
        in_specs=[vmem] * (6 + len(near)),
        out_specs=[vmem] * 3,
        scratch_shapes=[
            pltpu.VMEM(((bases + 3) * atoms, len(slots) * atoms), jnp.bfloat16),
            pltpu.VMEM((len(slots) * atoms, width), jnp.bfloat16),
        ],
        compiler_params=pltpu.CompilerParams(vmem_limit_bytes=40 * 1024 * 1024),
        name="pairs",
    )(
        offs,
        occ,
        mask[0, 0, 0].astype(jnp.float32)[None, :],
        targets[0, 0, 0],
        radial,
        readout[None, :],
        *near,
    )
    back = collect([mine] + [theirs[k] for k in range(len(steps_y) - 1)], "gy")
    back = back.reshape(len(steps_x), len(steps_z), width, atoms)
    back = collect([back[k] for k in range(len(steps_x))], "gx")
    back = collect([back[k] for k in range(len(steps_z))], "gz")
    grad = lax.dot_general(
        back, w_in, (((0,), (1,)), ((), ())), preferred_element_type=jnp.float32
    )
    return (pred.reshape(1, 1, 1, 3, atoms), grad.reshape(1, 1, 1, atoms, width))


def solution(mesh):
    in_specs = (
        P("gx", "gy", "gz", None, None),
        P("gx", "gy", "gz", None, None),
        P("gx", "gy", "gz"),
        P("gx", "gy", "gz", None),
        P("gx", "gy", "gz", None, None),
        P(),
        P(),
        P(),
    )
    out_specs = (P("gx", "gy", "gz", None, None), P("gx", "gy", "gz", None, None))
    return jax.shard_map(
        on_device, mesh=mesh, in_specs=in_specs, out_specs=out_specs, check_vma=False
    )
```

```python
import functools
import itertools
import math

import jax
import jax.numpy as jnp
from jax import lax
from jax.experimental import pallas as pl
from jax.experimental.pallas import tpu as pltpu
from jax.sharding import PartitionSpec as P

EDGE = 10.0
CUT = 5.0
GAMMA = 20.0
LOSS_WEIGHT = 16.0
FAR = 1000.0
TAIL = 16


def steps_of(size):
    return (0, None) if size == 2 else (0, -1, 1)


def shift(block, axis, step):
    size = lax.axis_size(axis)
    return lax.ppermute(block, axis, [(i, (i + step) % size) for i in range(size)])


def spread(blocks, axis):
    parts = [blocks]
    for step in steps_of(lax.axis_size(axis))[1:]:
        parts.append(shift(blocks, axis, 1 if step is None else -step))
    return parts


def collect(blocks, axis):
    total = blocks[0]
    for part, step in zip(blocks[1:], steps_of(lax.axis_size(axis))[1:]):
        total = total + shift(part, axis, 1 if step is None else step)
    return total


def occupied(counts_ref, atoms):
    return lax.broadcasted_iota(jnp.int32, (1, atoms), 1) < counts_ref[0]


def message_kernel(feat_ref, w_ref, offs_ref, counts_ref, out_ref):
    atoms, width = feat_ref.shape
    place = jnp.where(occupied(counts_ref, atoms), offs_ref[:, 0, :], -FAR)
    out_ref[:atoms, :] = jnp.dot(
        feat_ref[...], w_ref[...], preferred_element_type=jnp.float32
    ).astype(jnp.bfloat16)
    high = place.astype(jnp.bfloat16)
    rest = place - high.astype(jnp.float32)
    middle = rest.astype(jnp.bfloat16)
    low = (rest - middle.astype(jnp.float32)).astype(jnp.bfloat16)
    rows = jnp.concatenate(
        [
            high.astype(jnp.float32),
            middle.astype(jnp.float32),
            low.astype(jnp.float32),
            jnp.zeros((TAIL - 9, atoms), jnp.float32),
        ],
        0,
    )
    out_ref[atoms:, :atoms] = rows.astype(jnp.bfloat16)
    if width > atoms:
        out_ref[atoms:, atoms:] = jnp.zeros((TAIL, width - atoms), jnp.bfloat16)


def across(row, count):
    return jnp.transpose(jnp.broadcast_to(row, (count, row.shape[1])))


def build(slots, bases, offs_ref, counts_ref, place_ref, blocks, kern_ref, proj_ref):
    atoms = offs_ref.shape[2]
    rate = 2.0 * GAMMA / (bases - 1)
    occ = occupied(counts_ref, atoms)
    own = [across(jnp.where(occ, offs_ref[c], FAR), atoms) for c in range(3)]
    turn = [None if axis is None else 1 - 2 * (place_ref[axis] & 1) for axis in (0, None, 1)]
    for s, steps in enumerate(slots):
        block = blocks[s]
        proj_ref[s * atoms : (s + 1) * atoms, :] = block[:atoms, :]
        coded = block[atoms:, :atoms].astype(jnp.float32)
        apart = []
        for c in range(3):
            spot = coded[c : c + 1, :] + coded[3 + c : 4 + c, :] + coded[6 + c : 7 + c, :]
            step = steps[c]
            if step is None:
                away = spot - own[c]
                apart.append(away + jnp.where(away < 0.0, EDGE, -EDGE))
            elif step == 0:
                apart.append(spot - own[c])
            elif isinstance(step, str):
                apart.append((spot + (turn[c] * int(step)).astype(jnp.float32) * EDGE) - own[c])
            else:
                apart.append((spot + step * EDGE) - own[c])
        ratio = (apart[0] * apart[0] + apart[1] * apart[1] + apart[2] * apart[2]) * (
            1.0 / (CUT * CUT)
        )
        ratio = jnp.minimum(ratio, 1.0)
        if steps == (0, 0, 0):
            same = lax.broadcasted_iota(jnp.int32, (atoms, atoms), 0) == lax.broadcasted_iota(
                jnp.int32, (atoms, atoms), 1
            )
            ratio = jnp.where(same, 1.0, ratio)
        envelope = jnp.square(1.0 - ratio)
        value = envelope * jnp.exp(-GAMMA * jnp.square(ratio))
        growth = jnp.exp(rate * ratio)
        lanes = slice(s * atoms, (s + 1) * atoms)
        for b in range(bases):
            kern_ref[b * atoms : (b + 1) * atoms, lanes] = value.astype(jnp.bfloat16)
            if b + 1 < bases:
                value = value * growth
        envelope = envelope * (1.0 / CUT)
        for c in range(3):
            kern_ref[(bases + c) * atoms : (bases + c + 1) * atoms, lanes] = (
                envelope * apart[c]
            ).astype(jnp.bfloat16)


def gather(kern_ref, proj_ref):
    rows = kern_ref.shape[0] // 3
    return [
        jnp.dot(kern_ref[m * rows : (m + 1) * rows, :], proj_ref[...], preferred_element_type=jnp.float32)
        for m in range(3)
    ]


def scatter(right, kern_ref, held_ref, other_refs):
    atoms = held_ref.shape[2]
    ways = 1 + len(other_refs)
    for k in range(held_ref.shape[0]):
        lanes = slice(k * ways * atoms, (k + 1) * ways * atoms)
        back = lax.dot_general(
            right, kern_ref[:, lanes], (((0,), (0,)), ((), ())), preferred_element_type=jnp.float32
        )
        held_ref[k] = back[:, :atoms]
        for way, ref in enumerate(other_refs):
            ref[k] = back[:, (way + 1) * atoms : (way + 2) * atoms].astype(jnp.bfloat16)


def pick(refs, count, ways):
    return [refs[way].at[k] for k in range(count) for way in range(ways)]


def early_kernel(slots, ways, bases, offs_ref, counts_ref, place_ref, *refs):
    near, (kern_ref, msg_ref, proj_ref) = refs[:ways], refs[ways:]
    blocks = pick(near, len(slots) // ways, ways)
    build(slots, bases, offs_ref, counts_ref, place_ref, blocks, kern_ref, proj_ref)
    rows = kern_ref.shape[0] // 3
    for m, part in enumerate(gather(kern_ref, proj_ref)):
        msg_ref[m * rows : (m + 1) * rows, :] = part


def main_kernel(slots, ways, bases, early, offs_ref, counts_ref, place_ref, mask_ref, targ_ref, radial_ref, readout_ref, *refs):
    near, refs = refs[:ways], refs[ways:]
    if early:
        before_ref, pred_ref, right_ref, held_ref = refs[:4]
        refs = refs[4:]
    else:
        pred_ref, held_ref = refs[:2]
        refs = refs[2:]
    others, (kern_ref, proj_ref) = refs[: ways - 1], refs[ways - 1 :]
    atoms = offs_ref.shape[2]
    width = radial_ref.shape[1]
    blocks = pick(near, len(slots) // ways, ways)
    build(slots, bases, offs_ref, counts_ref, place_ref, blocks, kern_ref, proj_ref)
    msg = jnp.concatenate(gather(kern_ref, proj_ref), 0)
    if early:
        msg = msg + before_ref[...]
    fold = [math.exp(-GAMMA * (b / (bases - 1)) ** 2) for b in range(bases)]
    weight = [radial_ref[b : b + 1, :] * fold[b] for b in range(bases)]
    pre = weight[0] * msg[:atoms]
    for b in range(1, bases):
        pre = pre + weight[b] * msg[b * atoms : (b + 1) * atoms]
    gate = 1.0 / (1.0 + jnp.exp(-pre))
    readout = readout_ref[...]
    gates = readout * gate
    vec = [msg[(bases + c) * atoms : (bases + c + 1) * atoms] for c in range(3)]
    chosen = jnp.where(occupied(counts_ref, atoms), mask_ref[...].astype(jnp.float32), 0.0)
    lean = jnp.zeros((atoms, width), jnp.float32)
    sides = []
    for c in range(3):
        pred = jnp.sum(gates * vec[c], axis=1, keepdims=True)
        pred = jnp.transpose(jnp.broadcast_to(pred, (atoms, atoms)))[0:1, :]
        pred_ref[c] = pred
        err = across(LOSS_WEIGHT * chosen * (pred - targ_ref[c]), width)
        lean = lean + err * vec[c]
        sides.append((err * gates).astype(jnp.bfloat16))
    slope = lean * readout * gate * (1.0 - gate)
    right = jnp.concatenate([(weight[b] * slope).astype(jnp.bfloat16) for b in range(bases)] + sides, 0)
    if early:
        right_ref[...] = right
    scatter(right, kern_ref, held_ref, others)


def late_kernel(right_ref, kern_ref, held_ref, *other_refs):
    scatter(right_ref[...], kern_ref, held_ref, other_refs)


VMEM = pl.BlockSpec(memory_space=pltpu.VMEM)
SMEM = pl.BlockSpec(memory_space=pltpu.SMEM)
LIMIT = pltpu.CompilerParams(vmem_limit_bytes=40 * 1024 * 1024)


def struct(*shape, dtype=jnp.bfloat16):
    return jax.ShapeDtypeStruct(shape, dtype)


def products(count, ways, width, atoms):
    return [struct(count, width, atoms, dtype=jnp.float32)] + [struct(count, width, atoms)] * (ways - 1)


def call_early(slots, ways, bases, common, near):
    atoms, width = near[0].shape[1] - TAIL, near[0].shape[2]
    rows, columns = (bases + 3) * atoms, len(slots) * atoms
    return pl.pallas_call(
        functools.partial(early_kernel, slots, ways, bases),
        out_shape=[struct(rows, columns), struct(rows, width, dtype=jnp.float32)],
        in_specs=[VMEM, SMEM, SMEM] + [VMEM] * ways,
        out_specs=[VMEM] * 2,
        scratch_shapes=[pltpu.VMEM((columns, width), jnp.bfloat16)],
        compiler_params=LIMIT,
        cost_estimate=pl.CostEstimate(
            flops=2 * rows * columns * width, bytes_accessed=2 * rows * columns, transcendentals=2 * atoms * columns
        ),
        name="early",
    )(*common, *near)


def call_main(slots, ways, bases, common, readouts, near, before=None):
    atoms, width = near[0].shape[1] - TAIL, near[0].shape[2]
    rows, columns = (bases + 3) * atoms, len(slots) * atoms
    early = [] if before is None else [before]
    out_shape = [struct(3, 1, atoms, dtype=jnp.float32)]
    if early:
        out_shape.append(struct(rows, width))
    out_shape += products(len(slots) // ways, ways, width, atoms)
    return pl.pallas_call(
        functools.partial(main_kernel, slots, ways, bases, bool(early)),
        out_shape=out_shape,
        in_specs=[VMEM, SMEM, SMEM] + [VMEM] * (len(readouts) + ways + len(early)),
        out_specs=[VMEM] * len(out_shape),
        scratch_shapes=[pltpu.VMEM((rows, columns), jnp.bfloat16), pltpu.VMEM((columns, width), jnp.bfloat16)],
        compiler_params=LIMIT,
        name="main",
    )(*common, *readouts, *near, *early)


def call_late(right, kern, ways, atoms):
    rows, width = right.shape
    columns = kern.shape[1]
    out_shape = products(columns // (ways * atoms), ways, width, atoms)
    return pl.pallas_call(
        late_kernel,
        out_shape=out_shape,
        in_specs=[VMEM] * 2,
        out_specs=[VMEM] * len(out_shape),
        compiler_params=LIMIT,
        cost_estimate=pl.CostEstimate(flops=2 * rows * columns * width, bytes_accessed=2 * rows * columns, transcendentals=0),
        name="late",
    )(right, kern)


AXES = ("gx", "gy", "gz")


def swap(block, axis, flip):
    sizes = [lax.axis_size(a) for a in AXES]
    pairs = []
    for place in itertools.product(*(range(n) for n in sizes)):
        other = [p ^ flip if a == axis else p for a, p in zip(AXES, place)]
        other[1] = other[1] ^ 1
        pairs.append(tuple((q[0] * sizes[1] + q[1]) * sizes[2] + q[2] for q in (place, other)))
    return lax.ppermute(block, AXES, pairs)


def core(block):
    return lax.ppermute(block, "gy", [(0, 1), (1, 0)])


def narrow(block):
    return block.astype(jnp.bfloat16)


def exchange_small(message, bases, common, readouts):
    atoms = message.shape[0] - TAIL
    x1 = swap(message, "gx", 1)
    z1 = swap(message, "gz", 1)
    z3 = swap(message, "gz", 3)
    x3 = swap(x1, "gx", 2)
    x1z1 = swap(z1, "gx", 1)
    x3z1 = swap(x1z1, "gx", 2)
    x1z3 = swap(z3, "gx", 1)
    x3z3 = swap(x1z3, "gx", 2)
    near = jnp.stack([message, x1, x3, z1, z3])
    near_other = core(near)
    far = jnp.stack([x1z1, x3z1, x1z3, x3z3])
    far_other = core(far)

    def both(x, z, hops):
        held, other = (0, None) if hops % 2 == 0 else (None, 0)
        return [(x, held, z), (x, other, z)]

    near_slots = both(0, 0, 0) + both("1", 0, 1) + both("-1", 0, 2) + both(0, "1", 1) + both(0, "-1", 1)
    far_slots = both("1", "1", 2) + both("-1", "1", 3) + both("1", "-1", 2) + both("-1", "-1", 3)
    kern, before = call_early(near_slots, 2, bases, common, [near, near_other])
    pred, right, far_held, far_sent = call_main(far_slots, 2, bases, common, readouts, [far, far_other], before)
    far_sum = far_held + core(far_sent)
    near_held, near_sent = call_late(right, kern, 2, atoms)
    near_sum = near_held + core(near_sent)
    back3 = swap(narrow(far_sum[3]), "gx", 2)
    back1 = swap(narrow(far_sum[1]), "gx", 2)
    back3 = swap(narrow(far_sum[2] + back3), "gx", 1)
    back1 = swap(narrow(far_sum[0] + back1), "gx", 1)
    back0 = swap(narrow(near_sum[2]), "gx", 2)
    back3 = swap(narrow(near_sum[4] + back3), "gz", 3)
    back1 = swap(narrow(near_sum[3] + back1), "gz", 1)
    back0 = swap(narrow(near_sum[1] + back0), "gx", 1)
    return pred, near_sum[0] + back0 + back1 + back3


def exchange_any(message, bases, common, readouts):
    steps_x, steps_y, steps_z = (steps_of(lax.axis_size(a)) for a in AXES)
    near = jnp.concatenate(spread(message[None], "gz"), 0)
    near = jnp.concatenate(spread(near, "gx"), 0)
    near = spread(near, "gy")
    slots = [(x, y, z) for x, z, y in itertools.product(steps_x, steps_z, steps_y)]
    pred, *parts = call_main(slots, len(near), bases, common, readouts, near)
    back = collect(parts, "gy")
    back = back.reshape(len(steps_x), len(steps_z), *back.shape[1:])
    back = collect([back[0]] + [narrow(back[k]) for k in range(1, len(steps_x))], "gx")
    return pred, collect([back[0]] + [narrow(back[k]) for k in range(1, len(steps_z))], "gz")


def on_device(offsets, features, counts, mask, targets, w_in, radial, readout):
    atoms = features.shape[3]
    width = features.shape[4]
    bases = radial.shape[0]
    offs = offsets.reshape(3, 1, atoms)
    count = counts.reshape(1)
    place = jnp.stack([lax.axis_index("gx"), lax.axis_index("gz")]).astype(jnp.int32)
    message = pl.pallas_call(
        message_kernel,
        out_shape=struct(atoms + TAIL, width),
        in_specs=[VMEM, VMEM, VMEM, SMEM],
        out_specs=VMEM,
        name="message",
    )(features[0, 0, 0], w_in, offs, count)
    common = [offs, count, place]
    readouts = [mask.reshape(1, atoms), targets.reshape(3, 1, atoms), radial, readout[None, :]]
    small = tuple(lax.axis_size(a) for a in AXES) == (4, 2, 4)
    pred, back = (exchange_small if small else exchange_any)(message, bases, common, readouts)
    grad = lax.dot_general(
        narrow(back), w_in, (((0,), (1,)), ((), ())), preferred_element_type=jnp.float32
    )
    return (pred.reshape(1, 1, 1, 3, atoms), grad.reshape(1, 1, 1, atoms, width))


def solution(mesh):
    in_specs = (
        P("gx", "gy", "gz", None, None),
        P("gx", "gy", "gz", None, None),
        P("gx", "gy", "gz"),
        P("gx", "gy", "gz", None),
        P("gx", "gy", "gz", None, None),
        P(),
        P(),
        P(),
    )
    out_specs = (P("gx", "gy", "gz", None, None), P("gx", "gy", "gz", None, None))
    return jax.shard_map(
        on_device, mesh=mesh, in_specs=in_specs, out_specs=out_specs, check_vma=False
    )
```

```python
import functools
import itertools
import math

import jax
import jax.numpy as jnp
from jax import lax
from jax.experimental import pallas as pl
from jax.experimental.pallas import tpu as pltpu
from jax.sharding import PartitionSpec as P

EDGE = 10.0
CUT = 5.0
GAMMA = 20.0
LOSS_WEIGHT = 16.0
FAR = 1000.0
TAIL = 16


def steps_of(size):
    return (0, None) if size == 2 else (0, -1, 1)


def shift(block, axis, step):
    size = lax.axis_size(axis)
    return lax.ppermute(block, axis, [(i, (i + step) % size) for i in range(size)])


def spread(blocks, axis):
    parts = [blocks]
    for step in steps_of(lax.axis_size(axis))[1:]:
        parts.append(shift(blocks, axis, 1 if step is None else -step))
    return parts


def collect(blocks, axis):
    total = blocks[0]
    for part, step in zip(blocks[1:], steps_of(lax.axis_size(axis))[1:]):
        total = total + shift(part, axis, 1 if step is None else step)
    return total


def occupied(counts_ref, atoms):
    return lax.broadcasted_iota(jnp.int32, (1, atoms), 1) < counts_ref[...]


def message_kernel(feat_ref, w_ref, offs_ref, counts_ref, out_ref):
    atoms, width = feat_ref.shape
    place = jnp.where(occupied(counts_ref, atoms), offs_ref[:, 0, :], -FAR)
    out_ref[:atoms, :] = jnp.dot(
        feat_ref[...], w_ref[...], preferred_element_type=jnp.float32
    ).astype(jnp.bfloat16)
    high = place.astype(jnp.bfloat16)
    rest = place - high.astype(jnp.float32)
    middle = rest.astype(jnp.bfloat16)
    low = (rest - middle.astype(jnp.float32)).astype(jnp.bfloat16)
    rows = jnp.concatenate(
        [
            high.astype(jnp.float32),
            middle.astype(jnp.float32),
            low.astype(jnp.float32),
            jnp.zeros((TAIL - 9, atoms), jnp.float32),
        ],
        0,
    )
    out_ref[atoms:, :atoms] = rows.astype(jnp.bfloat16)
    if width > atoms:
        out_ref[atoms:, atoms:] = jnp.zeros((TAIL, width - atoms), jnp.bfloat16)


def across(row, count):
    return jnp.transpose(jnp.broadcast_to(row, (count, row.shape[1])))


def build(slots, bases, offs_ref, counts_ref, place_ref, blocks, kern_ref, proj_ref):
    atoms = offs_ref.shape[2]
    rate = 2.0 * GAMMA / (bases - 1)
    occ = occupied(counts_ref, atoms)
    own = [across(jnp.where(occ, offs_ref[c], FAR), atoms) for c in range(3)]
    turn = [None if axis is None else 1 - 2 * (place_ref[axis] & 1) for axis in (0, None, 1)]
    for s, steps in enumerate(slots):
        block = blocks[s]
        proj_ref[s * atoms : (s + 1) * atoms, :] = block[:atoms, :]
        coded = block[atoms:, :atoms].astype(jnp.float32)
        apart = []
        for c in range(3):
            spot = coded[c : c + 1, :] + coded[3 + c : 4 + c, :] + coded[6 + c : 7 + c, :]
            step = steps[c]
            if step is None:
                away = spot - own[c]
                apart.append(away + jnp.where(away < 0.0, EDGE, -EDGE))
            elif step == 0:
                apart.append(spot - own[c])
            elif isinstance(step, str):
                apart.append((spot + (turn[c] * int(step)).astype(jnp.float32) * EDGE) - own[c])
            else:
                apart.append((spot + step * EDGE) - own[c])
        ratio = (apart[0] * apart[0] + apart[1] * apart[1] + apart[2] * apart[2]) * (
            1.0 / (CUT * CUT)
        )
        ratio = jnp.minimum(ratio, 1.0)
        if steps == (0, 0, 0):
            same = lax.broadcasted_iota(jnp.int32, (atoms, atoms), 0) == lax.broadcasted_iota(
                jnp.int32, (atoms, atoms), 1
            )
            ratio = jnp.where(same, 1.0, ratio)
        envelope = jnp.square(1.0 - ratio)
        value = envelope * jnp.exp(-GAMMA * jnp.square(ratio))
        growth = jnp.exp(rate * ratio)
        lanes = slice(s * atoms, (s + 1) * atoms)
        for b in range(bases):
            kern_ref[b * atoms : (b + 1) * atoms, lanes] = value.astype(jnp.bfloat16)
            if b + 1 < bases:
                value = value * growth
        envelope = envelope * (1.0 / CUT)
        for c in range(3):
            kern_ref[(bases + c) * atoms : (bases + c + 1) * atoms, lanes] = (
                envelope * apart[c]
            ).astype(jnp.bfloat16)


def gather(kern_ref, proj_ref):
    rows = kern_ref.shape[0] // 3
    return [
        jnp.dot(kern_ref[m * rows : (m + 1) * rows, :], proj_ref[...], preferred_element_type=jnp.float32)
        for m in range(3)
    ]


def scatter(right, kern_ref, held_ref, other_refs):
    atoms = held_ref.shape[2]
    ways = 1 + len(other_refs)
    for k in range(held_ref.shape[0]):
        lanes = slice(k * ways * atoms, (k + 1) * ways * atoms)
        back = lax.dot_general(
            right, kern_ref[:, lanes], (((0,), (0,)), ((), ())), preferred_element_type=jnp.float32
        )
        held_ref[k] = back[:, :atoms]
        for way, ref in enumerate(other_refs):
            ref[k] = back[:, (way + 1) * atoms : (way + 2) * atoms].astype(jnp.bfloat16)


def pick(refs, ways):
    groups = [refs[g : g + ways] for g in range(0, len(refs), ways)]
    return [ref.at[k] for group in groups for k in range(group[0].shape[0]) for ref in group]


def early_kernel(slots, ways, bases, offs_ref, counts_ref, place_ref, *refs):
    near, (kern_ref, msg_ref, proj_ref) = refs[:-3], refs[-3:]
    blocks = pick(near, ways)
    build(slots, bases, offs_ref, counts_ref, place_ref, blocks, kern_ref, proj_ref)
    rows = kern_ref.shape[0] // 3
    for m, part in enumerate(gather(kern_ref, proj_ref)):
        msg_ref[m * rows : (m + 1) * rows, :] = part


def main_kernel(slots, ways, bases, arrays, early, offs_ref, counts_ref, place_ref, mask_ref, targ_ref, radial_ref, readout_ref, *refs):
    near, refs = refs[:arrays], refs[arrays:]
    if early:
        before_ref, pred_ref, right_ref, held_ref = refs[:4]
        refs = refs[4:]
    else:
        pred_ref, held_ref = refs[:2]
        refs = refs[2:]
    others, (kern_ref, proj_ref) = refs[: ways - 1], refs[ways - 1 :]
    atoms = offs_ref.shape[2]
    width = radial_ref.shape[1]
    blocks = pick(near, ways)
    build(slots, bases, offs_ref, counts_ref, place_ref, blocks, kern_ref, proj_ref)
    msg = jnp.concatenate(gather(kern_ref, proj_ref), 0)
    if early:
        msg = msg + before_ref[...]
    fold = [math.exp(-GAMMA * (b / (bases - 1)) ** 2) for b in range(bases)]
    weight = [radial_ref[b : b + 1, :] * fold[b] for b in range(bases)]
    pre = weight[0] * msg[:atoms]
    for b in range(1, bases):
        pre = pre + weight[b] * msg[b * atoms : (b + 1) * atoms]
    gate = 1.0 / (1.0 + jnp.exp(-pre))
    readout = readout_ref[...]
    gates = readout * gate
    vec = [msg[(bases + c) * atoms : (bases + c + 1) * atoms] for c in range(3)]
    chosen = jnp.where(occupied(counts_ref, atoms), mask_ref[...].astype(jnp.float32), 0.0)
    lean = jnp.zeros((atoms, width), jnp.float32)
    sides = []
    for c in range(3):
        pred = jnp.sum(gates * vec[c], axis=1, keepdims=True)
        pred = jnp.transpose(jnp.broadcast_to(pred, (atoms, atoms)))[0:1, :]
        pred_ref[c] = pred
        err = across(LOSS_WEIGHT * chosen * (pred - targ_ref[c]), width)
        lean = lean + err * vec[c]
        sides.append((err * gates).astype(jnp.bfloat16))
    slope = lean * readout * gate * (1.0 - gate)
    right = jnp.concatenate([(weight[b] * slope).astype(jnp.bfloat16) for b in range(bases)] + sides, 0)
    if early:
        right_ref[...] = right
    scatter(right, kern_ref, held_ref, others)


def late_kernel(right_ref, kern_ref, held_ref, *other_refs):
    scatter(right_ref[...], kern_ref, held_ref, other_refs)


VMEM = pl.BlockSpec(memory_space=pltpu.VMEM)
SMEM = pl.BlockSpec(memory_space=pltpu.SMEM)
LIMIT = pltpu.CompilerParams(vmem_limit_bytes=40 * 1024 * 1024)


def struct(*shape, dtype=jnp.bfloat16):
    return jax.ShapeDtypeStruct(shape, dtype)


def products(count, ways, width, atoms):
    return [struct(count, width, atoms, dtype=jnp.float32)] + [struct(count, width, atoms)] * (ways - 1)


def call_early(slots, ways, bases, common, near):
    atoms, width = near[0].shape[1] - TAIL, near[0].shape[2]
    rows, columns = (bases + 3) * atoms, len(slots) * atoms
    return pl.pallas_call(
        functools.partial(early_kernel, slots, ways, bases),
        out_shape=[struct(rows, columns), struct(rows, width, dtype=jnp.float32)],
        in_specs=[VMEM, VMEM, SMEM] + [VMEM] * len(near),
        out_specs=[VMEM] * 2,
        scratch_shapes=[pltpu.VMEM((columns, width), jnp.bfloat16)],
        compiler_params=LIMIT,
        cost_estimate=pl.CostEstimate(
            flops=10 * rows * columns * width, bytes_accessed=8 * rows * columns, transcendentals=2 * atoms * columns
        ),
        name="early",
    )(*common, *near)


def call_main(slots, ways, bases, common, readouts, near, before=None):
    atoms, width = near[0].shape[1] - TAIL, near[0].shape[2]
    rows, columns = (bases + 3) * atoms, len(slots) * atoms
    early = [] if before is None else [before]
    out_shape = [struct(3, 1, atoms, dtype=jnp.float32)]
    if early:
        out_shape.append(struct(rows, width))
    out_shape += products(len(slots) // ways, ways, width, atoms)
    return pl.pallas_call(
        functools.partial(main_kernel, slots, ways, bases, len(near), bool(early)),
        out_shape=out_shape,
        in_specs=[VMEM, VMEM, SMEM] + [VMEM] * (len(readouts) + len(near) + len(early)),
        out_specs=[VMEM] * len(out_shape),
        scratch_shapes=[pltpu.VMEM((rows, columns), jnp.bfloat16), pltpu.VMEM((columns, width), jnp.bfloat16)],
        compiler_params=LIMIT,
        name="main",
    )(*common, *readouts, *near, *early)


def call_late(right, kern, ways, atoms):
    rows, width = right.shape
    columns = kern.shape[1]
    out_shape = products(columns // (ways * atoms), ways, width, atoms)
    return pl.pallas_call(
        late_kernel,
        out_shape=out_shape,
        in_specs=[VMEM] * 2,
        out_specs=[VMEM] * len(out_shape),
        compiler_params=LIMIT,
        cost_estimate=pl.CostEstimate(flops=2 * rows * columns * width, bytes_accessed=2 * rows * columns, transcendentals=0),
        name="late",
    )(right, kern)


AXES = ("gx", "gy", "gz")


def swap(block, axis, flip):
    sizes = [lax.axis_size(a) for a in AXES]
    pairs = []
    for place in itertools.product(*(range(n) for n in sizes)):
        other = [p ^ flip if a == axis else p for a, p in zip(AXES, place)]
        other[1] = other[1] ^ 1
        pairs.append(tuple((q[0] * sizes[1] + q[1]) * sizes[2] + q[2] for q in (place, other)))
    return lax.ppermute(block, AXES, pairs)


def core(block):
    return lax.ppermute(block, "gy", [(0, 1), (1, 0)])


def narrow(block):
    return block.astype(jnp.bfloat16)


def after(block, other):
    return lax.optimization_barrier((block, other))[0]


def exchange_small(message, bases, common, readouts):
    atoms = message.shape[0] - TAIL
    x1 = swap(message, "gx", 1)
    z1 = swap(message, "gz", 1)
    z3 = swap(message, "gz", 3)
    x3 = swap(x1, "gx", 2)
    x1z1 = swap(z1, "gx", 1)
    x3z1 = swap(x1z1, "gx", 2)
    x1z3 = swap(z3, "gx", 1)
    x3z3 = swap(x1z3, "gx", 2)
    near = jnp.stack([x1, x3, z1, z3])
    near = [message[None], core(message)[None], near, core(near)]

    def both(x, z, hops):
        held, other = (0, None) if hops % 2 == 0 else (None, 0)
        return [(x, held, z), (x, other, z)]

    near_slots = both(0, 0, 0) + both("1", 0, 1) + both("-1", 0, 2) + both(0, "1", 1) + both(0, "-1", 1)
    far_slots = both("1", "1", 2) + both("-1", "1", 3) + both("1", "-1", 2) + both("-1", "-1", 3)
    kern, before = call_early(near_slots, 2, bases, common, near)
    far1 = jnp.stack([x1z1, x3z1])
    far = [far1, core(far1)]
    x1z3, x3z3, _, _ = lax.optimization_barrier((x1z3, x3z3, far[1], before))
    far3 = jnp.stack([x1z3, x3z3])
    far += [far3, core(far3)]
    pred, right, far_held, far_sent = call_main(far_slots, 2, bases, common, readouts, far, before)
    far_sum = far_held + core(far_sent)
    near_held, near_sent = call_late(right, kern, 2, atoms)
    near_sum = near_held + core(near_sent)
    back3 = swap(narrow(far_sum[3]), "gx", 2)
    back1 = swap(narrow(jnp.stack([far_sum[1], near_sum[2]])), "gx", 2)
    next3 = narrow(far_sum[2] + back3)
    next1 = narrow(jnp.stack([far_sum[0], near_sum[1]]) + after(back1, next3))
    back3 = swap(next3, "gx", 1)
    back1 = swap(next1, "gx", 1)
    next3 = narrow(near_sum[4] + back3)
    back1 = after(back1, next3)
    next1 = narrow(near_sum[3] + back1[0])
    back3 = swap(next3, "gz", 3)
    return pred, near_sum[0] + back1[1] + swap(next1, "gz", 1) + back3


def exchange_any(message, bases, common, readouts):
    steps_x, steps_y, steps_z = (steps_of(lax.axis_size(a)) for a in AXES)
    near = jnp.concatenate(spread(message[None], "gz"), 0)
    near = jnp.concatenate(spread(near, "gx"), 0)
    near = spread(near, "gy")
    slots = [(x, y, z) for x, z, y in itertools.product(steps_x, steps_z, steps_y)]
    pred, *parts = call_main(slots, len(near), bases, common, readouts, near)
    back = collect(parts, "gy")
    back = back.reshape(len(steps_x), len(steps_z), *back.shape[1:])
    back = collect([back[0]] + [narrow(back[k]) for k in range(1, len(steps_x))], "gx")
    return pred, collect([back[0]] + [narrow(back[k]) for k in range(1, len(steps_z))], "gz")


def on_device(offsets, features, counts, mask, targets, w_in, radial, readout):
    atoms = features.shape[3]
    width = features.shape[4]
    bases = radial.shape[0]
    offs = offsets.reshape(3, 1, atoms)
    count = counts.reshape(1, 1)
    place = jnp.stack([lax.axis_index("gx"), lax.axis_index("gz")]).astype(jnp.int32)
    message = pl.pallas_call(
        message_kernel,
        out_shape=struct(atoms + TAIL, width),
        in_specs=[VMEM] * 4,
        out_specs=VMEM,
        name="message",
    )(features[0, 0, 0], w_in, offs, count)
    common = [offs, count, place]
    readouts = [mask.reshape(1, atoms), targets.reshape(3, 1, atoms), radial, readout[None, :]]
    small = tuple(lax.axis_size(a) for a in AXES) == (4, 2, 4)
    pred, back = (exchange_small if small else exchange_any)(message, bases, common, readouts)
    grad = lax.dot_general(
        narrow(back), w_in, (((0,), (1,)), ((), ())), preferred_element_type=jnp.float32
    )
    return (pred.reshape(1, 1, 1, 3, atoms), grad.reshape(1, 1, 1, atoms, width))


def solution(mesh):
    in_specs = (
        P("gx", "gy", "gz", None, None),
        P("gx", "gy", "gz", None, None),
        P("gx", "gy", "gz"),
        P("gx", "gy", "gz", None),
        P("gx", "gy", "gz", None, None),
        P(),
        P(),
        P(),
    )
    out_specs = (P("gx", "gy", "gz", None, None), P("gx", "gy", "gz", None, None))
    return jax.shard_map(
        on_device, mesh=mesh, in_specs=in_specs, out_specs=out_specs, check_vma=False
    )
```

```python
import functools
import itertools
import math

import jax
import jax.numpy as jnp
from jax import lax
from jax.experimental import pallas as pl
from jax.experimental.pallas import tpu as pltpu
from jax.sharding import PartitionSpec as P

EDGE = 10.0
CUT = 5.0
GAMMA = 20.0
LOSS_WEIGHT = 16.0
FAR = 1000.0
TAIL = 16


def steps_of(size):
    return (0, None) if size == 2 else (0, -1, 1)


def shift(block, axis, step):
    size = lax.axis_size(axis)
    return lax.ppermute(block, axis, [(i, (i + step) % size) for i in range(size)])


def spread(blocks, axis):
    parts = [blocks]
    for step in steps_of(lax.axis_size(axis))[1:]:
        parts.append(shift(blocks, axis, 1 if step is None else -step))
    return parts


def collect(blocks, axis):
    total = blocks[0]
    for part, step in zip(blocks[1:], steps_of(lax.axis_size(axis))[1:]):
        total = total + shift(part, axis, 1 if step is None else step)
    return total


def message_kernel(feat_ref, w_ref, offs_ref, counts_ref, out_ref):
    atoms, width = feat_ref.shape
    occupied = lax.broadcasted_iota(jnp.int32, (1, atoms), 1) < counts_ref[...]
    place = jnp.where(occupied, offs_ref[:, 0, :], -FAR)
    proj = jnp.dot(
        feat_ref[...], w_ref[...], preferred_element_type=jnp.float32
    ).astype(jnp.bfloat16)
    for half in range(width // atoms):
        out_ref[half * atoms : (half + 1) * atoms, :] = proj[:, half * atoms : (half + 1) * atoms]
    high = place.astype(jnp.bfloat16)
    rest = place - high.astype(jnp.float32)
    middle = rest.astype(jnp.bfloat16)
    low = (rest - middle.astype(jnp.float32)).astype(jnp.bfloat16)
    rows = jnp.concatenate(
        [
            high.astype(jnp.float32),
            middle.astype(jnp.float32),
            low.astype(jnp.float32),
            jnp.zeros((TAIL - 9, atoms), jnp.float32),
        ],
        0,
    )
    out_ref[width:, :] = rows.astype(jnp.bfloat16)


def across(row, count):
    return jnp.transpose(jnp.broadcast_to(row, (count, row.shape[1])))


def spots(block):
    coded = block[block.shape[0] - TAIL :, :].astype(jnp.float32)
    return [coded[c : c + 1, :] + coded[3 + c : 4 + c, :] + coded[6 + c : 7 + c, :] for c in range(3)]


def build(slots, bases, own, place_ref, blocks, kern_ref, proj_ref):
    rows, atoms = blocks[0].shape
    rate = 2.0 * GAMMA / (bases - 1)
    own = [across(jnp.where(spot < -0.5 * FAR, FAR, spot), atoms) for spot in spots(own)]
    turn = [None if axis is None else 1 - 2 * (place_ref[axis] & 1) for axis in (0, None, 1)]
    for s, steps in enumerate(slots):
        block = blocks[s]
        for half in range((rows - TAIL) // atoms):
            proj_ref[s * atoms : (s + 1) * atoms, half * atoms : (half + 1) * atoms] = block[
                half * atoms : (half + 1) * atoms, :
            ]
        apart = []
        for c, spot in enumerate(spots(block)):
            step = steps[c]
            if step is None:
                away = spot - own[c]
                apart.append(away + jnp.where(away < 0.0, EDGE, -EDGE))
            elif step == 0:
                apart.append(spot - own[c])
            elif isinstance(step, str):
                apart.append((spot + (turn[c] * int(step)).astype(jnp.float32) * EDGE) - own[c])
            else:
                apart.append((spot + step * EDGE) - own[c])
        ratio = (apart[0] * apart[0] + apart[1] * apart[1] + apart[2] * apart[2]) * (
            1.0 / (CUT * CUT)
        )
        ratio = jnp.minimum(ratio, 1.0)
        if steps == (0, 0, 0):
            same = lax.broadcasted_iota(jnp.int32, (atoms, atoms), 0) == lax.broadcasted_iota(
                jnp.int32, (atoms, atoms), 1
            )
            ratio = jnp.where(same, 1.0, ratio)
        envelope = jnp.square(1.0 - ratio)
        value = envelope * jnp.exp(-GAMMA * jnp.square(ratio))
        growth = jnp.exp(rate * ratio)
        lanes = slice(s * atoms, (s + 1) * atoms)
        for b in range(bases):
            kern_ref[b * atoms : (b + 1) * atoms, lanes] = value.astype(jnp.bfloat16)
            if b + 1 < bases:
                value = value * growth
        envelope = envelope * (1.0 / CUT)
        for c in range(3):
            kern_ref[(bases + c) * atoms : (bases + c + 1) * atoms, lanes] = (
                envelope * apart[c]
            ).astype(jnp.bfloat16)


def gather(kern_ref, proj_ref):
    rows = kern_ref.shape[0] // 3
    return [
        jnp.dot(kern_ref[m * rows : (m + 1) * rows, :], proj_ref[...], preferred_element_type=jnp.float32)
        for m in range(3)
    ]


def scatter(right, kern_ref, lane, held_ref, other_refs, columns):
    atoms = held_ref.shape[2]
    ways = 1 + len(other_refs)
    for k, column in enumerate(columns):
        lanes = slice(lane + k * ways * atoms, lane + (k + 1) * ways * atoms)
        back = lax.dot_general(
            right, kern_ref[:, lanes], (((0,), (0,)), ((), ())), preferred_element_type=jnp.float32
        )
        held_ref[column] = back[:, :atoms]
        for way, ref in enumerate(other_refs):
            ref[column] = back[:, (way + 1) * atoms : (way + 2) * atoms].astype(jnp.bfloat16)


def pick(refs, ways):
    groups = [refs[g : g + ways] for g in range(0, len(refs), ways)]
    return [ref.at[k] for group in groups for k in range(group[0].shape[0]) for ref in group]


def early_kernel(slots, ways, bases, own_ref, place_ref, *refs):
    near, (kern_ref, msg_ref, proj_ref) = refs[:-3], refs[-3:]
    build(slots, bases, own_ref.at[0], place_ref, pick((own_ref,) + near, ways), kern_ref, proj_ref)
    rows = kern_ref.shape[0] // 3
    for m, part in enumerate(gather(kern_ref, proj_ref)):
        msg_ref[m * rows : (m + 1) * rows, :] = part


def main_kernel(slots, ways, bases, arrays, early, own_ref, place_ref, mask_ref, targ_ref, radial_ref, readout_ref, *refs):
    near, refs = refs[:arrays], refs[arrays:]
    if early:
        before_ref, side_ref, pred_ref, right_ref, held_ref = refs[:5]
        refs = refs[5:]
    else:
        pred_ref, held_ref = refs[:2]
        refs = refs[2:]
    others, (kern_ref, proj_ref) = refs[: ways - 1], refs[ways - 1 :]
    own = own_ref.at[0]
    atoms = own.shape[1]
    width = radial_ref.shape[1]
    blocks = pick(near if early else (own_ref,) + near, ways)
    build(slots, bases, own, place_ref, blocks, kern_ref, proj_ref)
    msg = jnp.concatenate(gather(kern_ref, proj_ref), 0)
    if early:
        msg = msg + before_ref[...]
    fold = [math.exp(-GAMMA * (b / (bases - 1)) ** 2) for b in range(bases)]
    weight = [radial_ref[b : b + 1, :] * fold[b] for b in range(bases)]
    pre = weight[0] * msg[:atoms]
    for b in range(1, bases):
        pre = pre + weight[b] * msg[b * atoms : (b + 1) * atoms]
    gate = 1.0 / (1.0 + jnp.exp(-pre))
    readout = readout_ref[...]
    gates = readout * gate
    vec = [msg[(bases + c) * atoms : (bases + c + 1) * atoms] for c in range(3)]
    chosen = jnp.where(spots(own)[0] < -0.5 * FAR, 0.0, mask_ref[...].astype(jnp.float32))
    lean = jnp.zeros((atoms, width), jnp.float32)
    sides = []
    for c in range(3):
        pred = jnp.sum(gates * vec[c], axis=1, keepdims=True)
        pred = jnp.transpose(jnp.broadcast_to(pred, (atoms, atoms)))[0:1, :]
        pred_ref[c] = pred
        err = across(LOSS_WEIGHT * chosen * (pred - targ_ref[c]), width)
        lean = lean + err * vec[c]
        sides.append((err * gates).astype(jnp.bfloat16))
    slope = lean * readout * gate * (1.0 - gate)
    right = jnp.concatenate([(weight[b] * slope).astype(jnp.bfloat16) for b in range(bases)] + sides, 0)
    if early:
        right_ref[...] = right
    total, fresh = held_ref.shape[0], len(slots) // ways
    scatter(right, kern_ref, 0, held_ref, others, range(total - fresh, total))
    if early:
        lane = side_ref.shape[1] - (total - fresh) * ways * atoms
        scatter(right, side_ref, lane, held_ref, others, range(total - fresh))


def late_kernel(right_ref, kern_ref, held_ref, *other_refs):
    scatter(right_ref[...], kern_ref, 0, held_ref, other_refs, range(held_ref.shape[0]))


VMEM = pl.BlockSpec(memory_space=pltpu.VMEM)
SMEM = pl.BlockSpec(memory_space=pltpu.SMEM)
LIMIT = pltpu.CompilerParams(vmem_limit_bytes=40 * 1024 * 1024)


def struct(*shape, dtype=jnp.bfloat16):
    return jax.ShapeDtypeStruct(shape, dtype)


def products(count, ways, width, atoms):
    return [struct(count, width, atoms, dtype=jnp.float32)] + [struct(count, width, atoms)] * (ways - 1)


def call_early(slots, ways, bases, own, place, near):
    atoms, width = near[0].shape[2], near[0].shape[1] - TAIL
    rows, columns = (bases + 3) * atoms, len(slots) * atoms
    return pl.pallas_call(
        functools.partial(early_kernel, slots, ways, bases),
        out_shape=[struct(rows, columns), struct(rows, width, dtype=jnp.float32)],
        in_specs=[VMEM, SMEM] + [VMEM] * len(near),
        out_specs=[VMEM] * 2,
        scratch_shapes=[pltpu.VMEM((columns, width), jnp.bfloat16)],
        compiler_params=LIMIT,
        cost_estimate=pl.CostEstimate(
            flops=10 * rows * columns * width, bytes_accessed=8 * rows * columns, transcendentals=2 * atoms * columns
        ),
        name="early",
    )(own, place, *near)


def call_main(slots, ways, bases, own, place, readouts, near, before=(), side=0):
    atoms, width = near[0].shape[2], near[0].shape[1] - TAIL
    rows, columns = (bases + 3) * atoms, len(slots) * atoms
    early = list(before)
    out_shape = [struct(3, 1, atoms, dtype=jnp.float32)]
    if early:
        out_shape.append(struct(rows, width))
    out_shape += products(side + len(slots) // ways, ways, width, atoms)
    return pl.pallas_call(
        functools.partial(main_kernel, slots, ways, bases, len(near), bool(early)),
        out_shape=out_shape,
        in_specs=[VMEM, SMEM] + [VMEM] * (len(readouts) + len(near) + len(early)),
        out_specs=[VMEM] * len(out_shape),
        scratch_shapes=[pltpu.VMEM((rows, columns), jnp.bfloat16), pltpu.VMEM((columns, width), jnp.bfloat16)],
        compiler_params=LIMIT,
        name="main",
    )(own, place, *readouts, *near, *early)


def call_late(right, kern, count, ways, atoms):
    rows, width = right.shape
    columns = count * ways * atoms
    out_shape = products(count, ways, width, atoms)
    return pl.pallas_call(
        late_kernel,
        out_shape=out_shape,
        in_specs=[VMEM] * 2,
        out_specs=[VMEM] * len(out_shape),
        compiler_params=LIMIT,
        cost_estimate=pl.CostEstimate(flops=2 * rows * columns * width, bytes_accessed=2 * rows * columns, transcendentals=0),
        name="late",
    )(right, kern)


AXES = ("gx", "gy", "gz")


def swap(block, axis, flip):
    sizes = [lax.axis_size(a) for a in AXES]
    pairs = []
    for place in itertools.product(*(range(n) for n in sizes)):
        other = [p ^ flip if a == axis else p for a, p in zip(AXES, place)]
        other[1] = other[1] ^ 1
        pairs.append(tuple((q[0] * sizes[1] + q[1]) * sizes[2] + q[2] for q in (place, other)))
    return lax.ppermute(block, AXES, pairs)


def core(block):
    return lax.ppermute(block, "gy", [(0, 1), (1, 0)])


def narrow(block):
    return block.astype(jnp.bfloat16)


def after(block, other):
    return lax.optimization_barrier((block, other))[0]


def exchange_small(message, bases, place, readouts):
    atoms = message.shape[1]
    x1 = swap(message, "gx", 1)
    z1 = swap(message, "gz", 1)
    z3 = swap(message, "gz", 3)
    x3 = swap(after(x1, z1), "gx", 2)
    x1z1 = swap(z1, "gx", 1)
    x1z3 = swap(z3, "gx", 1)
    x3z1 = swap(x1z1, "gx", 2)
    x3z3 = swap(x1z3, "gx", 2)

    def both(x, z, hops):
        held, other = (0, None) if hops % 2 == 0 else (None, 0)
        return [(x, held, z), (x, other, z)]
    near_slots = both(0, 0, 0) + both("1", 0, 1) + both("-1", 0, 2) + both(0, "1", 1) + both(0, "-1", 1)
    near = jnp.stack([x1, x3, z1, z3])
    own, rest = message[None], [core(message)[None], near, core(after(near, x1z3))]
    side = jnp.stack([x1z1, x3z1])
    rest += [side, core(after(side, x1z3))]
    near_slots += both("1", "1", 2) + both("-1", "1", 3)
    far_slots = both("1", "-1", 2) + both("-1", "-1", 3)
    kern, before = call_early(near_slots, 2, bases, own, place, rest)
    x3z3 = after(x3z3, before)
    far = jnp.stack([x1z3, x3z3])
    far = [far, core(far)]
    pred, right, far_held, far_sent = call_main(far_slots, 2, bases, own, place, readouts, far, (before, kern), 2)
    far_sum = far_held + core(far_sent)
    near_held, near_sent = call_late(right, kern, 5, 2, atoms)
    near_sum = near_held + core(near_sent)
    back3 = swap(narrow(far_sum[3]), "gx", 2)
    back1 = swap(narrow(jnp.stack([far_sum[1], near_sum[2]])), "gx", 2)
    next3 = narrow(far_sum[2] + back3)
    back1 = after(back1, next3)
    next1 = narrow(far_sum[0] + back1[0])
    back0 = back1[1]
    next0 = narrow(near_sum[1] + back0)
    back3 = swap(next3, "gx", 1)
    back1 = swap(next1, "gx", 1)
    back0 = swap(next0, "gx", 1)
    next3 = narrow(near_sum[4] + back3)
    back1 = after(back1, next3)
    next1 = narrow(near_sum[3] + back1)
    back3 = swap(next3, "gz", 3)
    back1 = swap(next1, "gz", 1)
    return pred, near_sum[0] + back0 + back1 + back3


def exchange_any(message, bases, place, readouts):
    steps_x, steps_y, steps_z = (steps_of(lax.axis_size(a)) for a in AXES)
    near = jnp.concatenate(spread(message[None], "gz"), 0)
    near = jnp.concatenate(spread(near, "gx"), 0)
    near = spread(near, "gy")
    slots = [(x, y, z) for x, z, y in itertools.product(steps_x, steps_z, steps_y)]
    pred, *parts = call_main(slots, len(near), bases, near[0], place, readouts, near[1:])
    back = collect(parts, "gy")
    back = back.reshape(len(steps_x), len(steps_z), *back.shape[1:])
    back = collect([back[0]] + [narrow(back[k]) for k in range(1, len(steps_x))], "gx")
    return pred, collect([back[0]] + [narrow(back[k]) for k in range(1, len(steps_z))], "gz")


def on_device(offsets, features, counts, mask, targets, w_in, radial, readout):
    atoms = features.shape[3]
    width = features.shape[4]
    bases = radial.shape[0]
    offs = offsets.reshape(3, 1, atoms)
    count = counts.reshape(1, 1)
    place = jnp.stack([lax.axis_index("gx"), lax.axis_index("gz")]).astype(jnp.int32)
    message = pl.pallas_call(
        message_kernel,
        out_shape=struct(width + TAIL, atoms),
        in_specs=[VMEM] * 4,
        out_specs=VMEM,
        name="message",
    )(features[0, 0, 0], w_in, offs, count)
    readouts = [mask.reshape(1, atoms), targets.reshape(3, 1, atoms), radial, readout[None, :]]
    small = tuple(lax.axis_size(a) for a in AXES) == (4, 2, 4)
    pred, back = (exchange_small if small else exchange_any)(message, bases, place, readouts)
    grad = lax.dot_general(
        narrow(back), w_in, (((0,), (1,)), ((), ())), preferred_element_type=jnp.float32
    )
    return (pred.reshape(1, 1, 1, 3, atoms), grad.reshape(1, 1, 1, atoms, width))


def solution(mesh):
    in_specs = (
        P("gx", "gy", "gz", None, None),
        P("gx", "gy", "gz", None, None),
        P("gx", "gy", "gz"),
        P("gx", "gy", "gz", None),
        P("gx", "gy", "gz", None, None),
        P(),
        P(),
        P(),
    )
    out_specs = (P("gx", "gy", "gz", None, None), P("gx", "gy", "gz", None, None))
    return jax.shard_map(
        on_device, mesh=mesh, in_specs=in_specs, out_specs=out_specs, check_vma=False
    )
```

```python
import functools
import itertools
import math

import jax
import jax.numpy as jnp
from jax import lax
from jax.experimental import pallas as pl
from jax.experimental.pallas import tpu as pltpu
from jax.sharding import PartitionSpec as P

EDGE = 10.0
CUT = 5.0
GAMMA = 20.0
LOSS_WEIGHT = 16.0
FAR = 1000.0
TAIL = 16


def steps_of(size):
    return (0, None) if size == 2 else (0, -1, 1)


def shift(block, axis, step):
    size = lax.axis_size(axis)
    return lax.ppermute(block, axis, [(i, (i + step) % size) for i in range(size)])


def spread(blocks, axis):
    parts = [blocks]
    for step in steps_of(lax.axis_size(axis))[1:]:
        parts.append(shift(blocks, axis, 1 if step is None else -step))
    return parts


def collect(blocks, axis):
    total = blocks[0]
    for part, step in zip(blocks[1:], steps_of(lax.axis_size(axis))[1:]):
        total = total + shift(part, axis, 1 if step is None else step)
    return total


def message_kernel(feat_ref, w_ref, offs_ref, counts_ref, out_ref):
    atoms, width = feat_ref.shape
    occupied = lax.broadcasted_iota(jnp.int32, (1, atoms), 1) < counts_ref[...]
    place = jnp.where(occupied, offs_ref[:, 0, :], -FAR)
    proj = jnp.dot(
        feat_ref[...], w_ref[...], preferred_element_type=jnp.float32
    ).astype(jnp.bfloat16)
    for half in range(width // atoms):
        out_ref[half * atoms : (half + 1) * atoms, :] = proj[:, half * atoms : (half + 1) * atoms]
    high = place.astype(jnp.bfloat16)
    rest = place - high.astype(jnp.float32)
    middle = rest.astype(jnp.bfloat16)
    low = (rest - middle.astype(jnp.float32)).astype(jnp.bfloat16)
    rows = jnp.concatenate(
        [
            high.astype(jnp.float32),
            middle.astype(jnp.float32),
            low.astype(jnp.float32),
            jnp.zeros((TAIL - 9, atoms), jnp.float32),
        ],
        0,
    )
    out_ref[width:, :] = rows.astype(jnp.bfloat16)


def across(row, count):
    return jnp.transpose(jnp.broadcast_to(row, (count, row.shape[1])))


def spots(block):
    coded = block[block.shape[0] - TAIL :, :].astype(jnp.float32)
    return [coded[c : c + 1, :] + coded[3 + c : 4 + c, :] + coded[6 + c : 7 + c, :] for c in range(3)]


def build(slots, bases, own, place_ref, blocks, kern_ref, proj_ref):
    rows, atoms = blocks[0].shape
    rate = 2.0 * GAMMA / (bases - 1)
    own = [across(jnp.where(spot < -0.5 * FAR, FAR, spot), atoms) for spot in spots(own)]
    turn = [None if axis is None else 1 - 2 * (place_ref[axis] & 1) for axis in (0, None, 1)]
    for s, steps in enumerate(slots):
        block = blocks[s]
        for half in range((rows - TAIL) // atoms):
            proj_ref[s * atoms : (s + 1) * atoms, half * atoms : (half + 1) * atoms] = block[
                half * atoms : (half + 1) * atoms, :
            ]
        apart = []
        for c, spot in enumerate(spots(block)):
            step = steps[c]
            if step is None:
                away = spot - own[c]
                apart.append(away + jnp.where(away < 0.0, EDGE, -EDGE))
            elif step == 0:
                apart.append(spot - own[c])
            elif isinstance(step, str):
                apart.append((spot + (turn[c] * int(step)).astype(jnp.float32) * EDGE) - own[c])
            else:
                apart.append((spot + step * EDGE) - own[c])
        ratio = (apart[0] * apart[0] + apart[1] * apart[1] + apart[2] * apart[2]) * (
            1.0 / (CUT * CUT)
        )
        ratio = jnp.minimum(ratio, 1.0)
        if steps == (0, 0, 0):
            same = lax.broadcasted_iota(jnp.int32, (atoms, atoms), 0) == lax.broadcasted_iota(
                jnp.int32, (atoms, atoms), 1
            )
            ratio = jnp.where(same, 1.0, ratio)
        envelope = jnp.square(1.0 - ratio)
        value = envelope * jnp.exp(-GAMMA * jnp.square(ratio))
        growth = jnp.exp(rate * ratio)
        lanes = slice(s * atoms, (s + 1) * atoms)
        for b in range(bases):
            kern_ref[b * atoms : (b + 1) * atoms, lanes] = value.astype(jnp.bfloat16)
            if b + 1 < bases:
                value = value * growth
        envelope = envelope * (1.0 / CUT)
        for c in range(3):
            kern_ref[(bases + c) * atoms : (bases + c + 1) * atoms, lanes] = (
                envelope * apart[c]
            ).astype(jnp.bfloat16)


def gather(kern_ref, proj_ref):
    rows = kern_ref.shape[0] // 3
    return [
        jnp.dot(kern_ref[m * rows : (m + 1) * rows, :], proj_ref[...], preferred_element_type=jnp.float32)
        for m in range(3)
    ]


def scatter(right, kern_ref, lane, held_ref, other_refs, columns):
    atoms = held_ref.shape[2]
    ways = 1 + len(other_refs)
    for k, column in enumerate(columns):
        lanes = slice(lane + k * ways * atoms, lane + (k + 1) * ways * atoms)
        back = lax.dot_general(
            right, kern_ref[:, lanes], (((0,), (0,)), ((), ())), preferred_element_type=jnp.float32
        )
        held_ref[column] = back[:, :atoms]
        for way, ref in enumerate(other_refs):
            ref[column] = back[:, (way + 1) * atoms : (way + 2) * atoms].astype(jnp.bfloat16)


def pick(refs, ways):
    groups = [refs[g : g + ways] for g in range(0, len(refs), ways)]
    return [ref.at[k] for group in groups for k in range(group[0].shape[0]) for ref in group]


def early_kernel(slots, ways, bases, more, own_ref, place_ref, *refs):
    near, (kern_ref, msg_ref, proj_ref) = refs[:-3], refs[-3:]
    blocks = pick(near[1:] if more else (own_ref,) + near, ways)
    build(slots, bases, own_ref.at[0], place_ref, blocks, kern_ref, proj_ref)
    rows = kern_ref.shape[0] // 3
    for m, part in enumerate(gather(kern_ref, proj_ref)):
        if more:
            part = part + near[0][m * rows : (m + 1) * rows, :]
        msg_ref[m * rows : (m + 1) * rows, :] = part


def main_kernel(slots, ways, bases, arrays, early, own_ref, place_ref, mask_ref, targ_ref, radial_ref, readout_ref, *refs):
    near, refs = refs[:arrays], refs[arrays:]
    if early:
        before_ref, side_ref, pred_ref, right_ref, held_ref = refs[:5]
        refs = refs[5:]
    else:
        pred_ref, held_ref = refs[:2]
        refs = refs[2:]
    others, (kern_ref, proj_ref) = refs[: ways - 1], refs[ways - 1 :]
    own = own_ref.at[0]
    atoms = own.shape[1]
    width = radial_ref.shape[1]
    blocks = pick(near if early else (own_ref,) + near, ways)
    build(slots, bases, own, place_ref, blocks, kern_ref, proj_ref)
    msg = jnp.concatenate(gather(kern_ref, proj_ref), 0)
    if early:
        msg = msg + before_ref[...]
    fold = [math.exp(-GAMMA * (b / (bases - 1)) ** 2) for b in range(bases)]
    weight = [radial_ref[b : b + 1, :] * fold[b] for b in range(bases)]
    pre = weight[0] * msg[:atoms]
    for b in range(1, bases):
        pre = pre + weight[b] * msg[b * atoms : (b + 1) * atoms]
    gate = 1.0 / (1.0 + jnp.exp(-pre))
    readout = readout_ref[...]
    gates = readout * gate
    vec = [msg[(bases + c) * atoms : (bases + c + 1) * atoms] for c in range(3)]
    chosen = jnp.where(spots(own)[0] < -0.5 * FAR, 0.0, mask_ref[...].astype(jnp.float32))
    lean = jnp.zeros((atoms, width), jnp.float32)
    sides = []
    for c in range(3):
        pred = jnp.sum(gates * vec[c], axis=1, keepdims=True)
        pred = jnp.transpose(jnp.broadcast_to(pred, (atoms, atoms)))[0:1, :]
        pred_ref[c] = pred
        err = across(LOSS_WEIGHT * chosen * (pred - targ_ref[c]), width)
        lean = lean + err * vec[c]
        sides.append((err * gates).astype(jnp.bfloat16))
    slope = lean * readout * gate * (1.0 - gate)
    right = jnp.concatenate([(weight[b] * slope).astype(jnp.bfloat16) for b in range(bases)] + sides, 0)
    if early:
        right_ref[...] = right
    total, fresh = held_ref.shape[0], len(slots) // ways
    scatter(right, kern_ref, 0, held_ref, others, range(total - fresh, total))
    if early:
        lane = side_ref.shape[1] - (total - fresh) * ways * atoms
        scatter(right, side_ref, lane, held_ref, others, range(total - fresh))


def late_kernel(right_ref, kern_ref, held_ref, *other_refs):
    scatter(right_ref[...], kern_ref, 0, held_ref, other_refs, range(held_ref.shape[0]))


VMEM = pl.BlockSpec(memory_space=pltpu.VMEM)
SMEM = pl.BlockSpec(memory_space=pltpu.SMEM)
LIMIT = pltpu.CompilerParams(vmem_limit_bytes=40 * 1024 * 1024)


def struct(*shape, dtype=jnp.bfloat16):
    return jax.ShapeDtypeStruct(shape, dtype)


def products(count, ways, width, atoms):
    return [struct(count, width, atoms, dtype=jnp.float32)] + [struct(count, width, atoms)] * (ways - 1)


def call_early(slots, ways, bases, own, place, near, before=None):
    atoms, width = near[0].shape[2], near[0].shape[1] - TAIL
    rows, columns = (bases + 3) * atoms, len(slots) * atoms
    more = [] if before is None else [before]
    return pl.pallas_call(
        functools.partial(early_kernel, slots, ways, bases, bool(more)),
        out_shape=[struct(rows, columns), struct(rows, width, dtype=jnp.float32)],
        in_specs=[VMEM, SMEM] + [VMEM] * (len(more) + len(near)),
        out_specs=[VMEM] * 2,
        scratch_shapes=[pltpu.VMEM((columns, width), jnp.bfloat16)],
        compiler_params=LIMIT,
        cost_estimate=pl.CostEstimate(
            flops=10 * rows * columns * width, bytes_accessed=8 * rows * columns, transcendentals=2 * atoms * columns
        ),
        name="early" if before is None else "side",
    )(own, place, *more, *near)


def call_main(slots, ways, bases, own, place, readouts, near, before=(), side=0):
    atoms, width = near[0].shape[2], near[0].shape[1] - TAIL
    rows, columns = (bases + 3) * atoms, len(slots) * atoms
    early = list(before)
    out_shape = [struct(3, 1, atoms, dtype=jnp.float32)]
    if early:
        out_shape.append(struct(rows, width))
    out_shape += products(side + len(slots) // ways, ways, width, atoms)
    return pl.pallas_call(
        functools.partial(main_kernel, slots, ways, bases, len(near), bool(early)),
        out_shape=out_shape,
        in_specs=[VMEM, SMEM] + [VMEM] * (len(readouts) + len(near) + len(early)),
        out_specs=[VMEM] * len(out_shape),
        scratch_shapes=[pltpu.VMEM((rows, columns), jnp.bfloat16), pltpu.VMEM((columns, width), jnp.bfloat16)],
        compiler_params=LIMIT,
        name="main",
    )(own, place, *readouts, *near, *early)


def call_late(right, kern, count, ways, atoms):
    rows, width = right.shape
    columns = count * ways * atoms
    out_shape = products(count, ways, width, atoms)
    return pl.pallas_call(
        late_kernel,
        out_shape=out_shape,
        in_specs=[VMEM] * 2,
        out_specs=[VMEM] * len(out_shape),
        compiler_params=LIMIT,
        cost_estimate=pl.CostEstimate(flops=2 * rows * columns * width, bytes_accessed=2 * rows * columns, transcendentals=0),
        name="late",
    )(right, kern)


AXES = ("gx", "gy", "gz")


def swap(block, axis, flip):
    sizes = [lax.axis_size(a) for a in AXES]
    pairs = []
    for place in itertools.product(*(range(n) for n in sizes)):
        other = [p ^ flip if a == axis else p for a, p in zip(AXES, place)]
        other[1] = other[1] ^ 1
        pairs.append(tuple((q[0] * sizes[1] + q[1]) * sizes[2] + q[2] for q in (place, other)))
    return lax.ppermute(block, AXES, pairs)


def core(block):
    return lax.ppermute(block, "gy", [(0, 1), (1, 0)])


def narrow(block):
    return block.astype(jnp.bfloat16)


def after(block, other):
    return lax.optimization_barrier((block, other))[0]


def exchange_small(message, bases, place, readouts):
    atoms = message.shape[1]
    x1 = swap(message, "gx", 1)
    z1 = swap(message, "gz", 1)
    z3 = swap(message, "gz", 3)
    x3 = swap(x1, "gx", 2)
    x1z1 = swap(z1, "gx", 1)
    x1z3 = swap(z3, "gx", 1)
    x3z1 = swap(x1z1, "gx", 2)
    x3z3 = swap(x1z3, "gx", 2)

    def both(x, z, hops):
        held, other = (0, None) if hops % 2 == 0 else (None, 0)
        return [(x, held, z), (x, other, z)]
    near_slots = both(0, 0, 0) + both("1", 0, 1) + both("-1", 0, 2) + both(0, "1", 1) + both(0, "-1", 1)
    side_slots = both("1", "1", 2) + both("-1", "1", 3)
    far_slots = both("1", "-1", 2) + both("-1", "-1", 3)
    near = jnp.stack([x1, x3, z1, z3])
    echo = core(message[None])
    own, rest = core(echo), [echo, near, core(near)]
    kern, before = call_early(near_slots, 2, bases, own, place, rest)
    side = jnp.stack([x1z1, x3z1])
    side = [side, core(side)]
    x1z3, x3z3, _ = lax.optimization_barrier((x1z3, x3z3, before))
    side[0], side[1], _ = lax.optimization_barrier((side[0], side[1], x3z3))
    kern_side, before = call_early(side_slots, 2, bases, own, place, side, before)
    far = jnp.stack([x1z3, x3z3])
    far = [far, core(far)]
    pred, right, far_held, far_sent = call_main(far_slots, 2, bases, own, place, readouts, far, (before, kern_side), 2)
    far_sum = far_held + core(far_sent)
    near_held, near_sent = call_late(right, kern, 5, 2, atoms)
    near_sum = near_held + core(near_sent)
    back3 = swap(narrow(far_sum[3]), "gx", 2)
    back1 = swap(narrow(jnp.stack([far_sum[1], near_sum[2]])), "gx", 2)
    next3 = narrow(far_sum[2] + back3)
    back1 = after(back1, next3)
    next1 = narrow(far_sum[0] + back1[0])
    back0 = back1[1]
    next0 = narrow(near_sum[1] + back0)
    back3 = swap(next3, "gx", 1)
    back1 = swap(next1, "gx", 1)
    back0 = swap(next0, "gx", 1)
    next3 = narrow(near_sum[4] + back3)
    back1 = after(back1, next3)
    next1 = narrow(near_sum[3] + back1)
    back3 = swap(next3, "gz", 3)
    back1 = swap(next1, "gz", 1)
    return pred, near_sum[0] + back0 + back1 + back3


def exchange_any(message, bases, place, readouts):
    steps_x, steps_y, steps_z = (steps_of(lax.axis_size(a)) for a in AXES)
    near = jnp.concatenate(spread(message[None], "gz"), 0)
    near = jnp.concatenate(spread(near, "gx"), 0)
    near = spread(near, "gy")
    slots = [(x, y, z) for x, z, y in itertools.product(steps_x, steps_z, steps_y)]
    pred, *parts = call_main(slots, len(near), bases, near[0], place, readouts, near[1:])
    back = collect(parts, "gy")
    back = back.reshape(len(steps_x), len(steps_z), *back.shape[1:])
    back = collect([back[0]] + [narrow(back[k]) for k in range(1, len(steps_x))], "gx")
    return pred, collect([back[0]] + [narrow(back[k]) for k in range(1, len(steps_z))], "gz")


def on_device(offsets, features, counts, mask, targets, w_in, radial, readout):
    atoms = features.shape[3]
    width = features.shape[4]
    bases = radial.shape[0]
    offs = offsets.reshape(3, 1, atoms)
    count = counts.reshape(1, 1)
    place = jnp.stack([lax.axis_index("gx"), lax.axis_index("gz")]).astype(jnp.int32)
    message = pl.pallas_call(
        message_kernel,
        out_shape=struct(width + TAIL, atoms),
        in_specs=[VMEM] * 4,
        out_specs=VMEM,
        name="message",
    )(features[0, 0, 0], w_in, offs, count)
    readouts = [mask.reshape(1, atoms), targets.reshape(3, 1, atoms), radial, readout[None, :]]
    small = tuple(lax.axis_size(a) for a in AXES) == (4, 2, 4)
    pred, back = (exchange_small if small else exchange_any)(message, bases, place, readouts)
    grad = lax.dot_general(
        narrow(back), w_in, (((0,), (1,)), ((), ())), preferred_element_type=jnp.float32
    )
    return (pred.reshape(1, 1, 1, 3, atoms), grad.reshape(1, 1, 1, atoms, width))


def solution(mesh):
    in_specs = (
        P("gx", "gy", "gz", None, None),
        P("gx", "gy", "gz", None, None),
        P("gx", "gy", "gz"),
        P("gx", "gy", "gz", None),
        P("gx", "gy", "gz", None, None),
        P(),
        P(),
        P(),
    )
    out_specs = (P("gx", "gy", "gz", None, None), P("gx", "gy", "gz", None, None))
    return jax.shard_map(
        on_device, mesh=mesh, in_specs=in_specs, out_specs=out_specs, check_vma=False
    )
```

```python
import functools
import itertools
import math

import jax
import jax.numpy as jnp
from jax import lax
from jax.experimental import pallas as pl
from jax.experimental.pallas import tpu as pltpu
from jax.sharding import PartitionSpec as P

EDGE = 10.0
CUT = 5.0
GAMMA = 20.0
LOSS_WEIGHT = 16.0
FAR = 1000.0
TAIL = 16


def steps_of(size):
    return (0, None) if size == 2 else (0, -1, 1)


def shift(block, axis, step):
    size = lax.axis_size(axis)
    return lax.ppermute(block, axis, [(i, (i + step) % size) for i in range(size)])


def spread(blocks, axis):
    parts = [blocks]
    for step in steps_of(lax.axis_size(axis))[1:]:
        parts.append(shift(blocks, axis, 1 if step is None else -step))
    return parts


def collect(blocks, axis):
    total = blocks[0]
    for part, step in zip(blocks[1:], steps_of(lax.axis_size(axis))[1:]):
        total = total + shift(part, axis, 1 if step is None else step)
    return total


def message_kernel(feat_ref, w_ref, offs_ref, counts_ref, out_ref):
    atoms, width = feat_ref.shape
    occupied = lax.broadcasted_iota(jnp.int32, (1, atoms), 1) < counts_ref[...]
    place = jnp.where(occupied, offs_ref[:, 0, :], -FAR)
    proj = jnp.dot(
        feat_ref[...], w_ref[...], preferred_element_type=jnp.float32
    ).astype(jnp.bfloat16)
    for half in range(width // atoms):
        out_ref[half * atoms : (half + 1) * atoms, :] = proj[:, half * atoms : (half + 1) * atoms]
    high = place.astype(jnp.bfloat16)
    rest = place - high.astype(jnp.float32)
    middle = rest.astype(jnp.bfloat16)
    low = (rest - middle.astype(jnp.float32)).astype(jnp.bfloat16)
    rows = jnp.concatenate(
        [
            high.astype(jnp.float32),
            middle.astype(jnp.float32),
            low.astype(jnp.float32),
            jnp.zeros((TAIL - 9, atoms), jnp.float32),
        ],
        0,
    )
    out_ref[width:, :] = rows.astype(jnp.bfloat16)


def across(row, count):
    return jnp.transpose(jnp.broadcast_to(row, (count, row.shape[1])))


def spots(block):
    coded = block[block.shape[0] - TAIL :, :].astype(jnp.float32)
    return [coded[c : c + 1, :] + coded[3 + c : 4 + c, :] + coded[6 + c : 7 + c, :] for c in range(3)]


def build(slots, bases, own, place_ref, blocks, kern_ref, proj_ref):
    rows, atoms = blocks[0].shape
    rate = 2.0 * GAMMA / (bases - 1)
    own = [across(jnp.where(spot < -0.5 * FAR, FAR, spot), atoms) for spot in spots(own)]
    turn = [None if axis is None else 1 - 2 * (place_ref[axis] & 1) for axis in (0, None, 1)]
    for s, steps in enumerate(slots):
        block = blocks[s]
        for half in range((rows - TAIL) // atoms):
            proj_ref[s * atoms : (s + 1) * atoms, half * atoms : (half + 1) * atoms] = block[
                half * atoms : (half + 1) * atoms, :
            ]
        apart = []
        for c, spot in enumerate(spots(block)):
            step = steps[c]
            if step is None:
                away = spot - own[c]
                apart.append(away + jnp.where(away < 0.0, EDGE, -EDGE))
            elif step == 0:
                apart.append(spot - own[c])
            elif isinstance(step, str):
                apart.append((spot + (turn[c] * int(step)).astype(jnp.float32) * EDGE) - own[c])
            else:
                apart.append((spot + step * EDGE) - own[c])
        ratio = (apart[0] * apart[0] + apart[1] * apart[1] + apart[2] * apart[2]) * (
            1.0 / (CUT * CUT)
        )
        ratio = jnp.minimum(ratio, 1.0)
        if steps == (0, 0, 0):
            same = lax.broadcasted_iota(jnp.int32, (atoms, atoms), 0) == lax.broadcasted_iota(
                jnp.int32, (atoms, atoms), 1
            )
            ratio = jnp.where(same, 1.0, ratio)
        envelope = jnp.square(1.0 - ratio)
        value = envelope * jnp.exp(-GAMMA * jnp.square(ratio))
        growth = jnp.exp(rate * ratio)
        lanes = slice(s * atoms, (s + 1) * atoms)
        for b in range(bases):
            kern_ref[b * atoms : (b + 1) * atoms, lanes] = value.astype(jnp.bfloat16)
            if b + 1 < bases:
                value = value * growth
        envelope = envelope * (1.0 / CUT)
        for c in range(3):
            kern_ref[(bases + c) * atoms : (bases + c + 1) * atoms, lanes] = (
                envelope * apart[c]
            ).astype(jnp.bfloat16)


def gather(kern_ref, proj_ref):
    rows = kern_ref.shape[0] // 3
    return [
        jnp.dot(kern_ref[m * rows : (m + 1) * rows, :], proj_ref[...], preferred_element_type=jnp.float32)
        for m in range(3)
    ]


def scatter(right, kern_ref, lane, held_ref, other_refs, columns):
    atoms = held_ref.shape[2]
    ways = 1 + len(other_refs)
    for k, column in enumerate(columns):
        lanes = slice(lane + k * ways * atoms, lane + (k + 1) * ways * atoms)
        back = lax.dot_general(
            right, kern_ref[:, lanes], (((0,), (0,)), ((), ())), preferred_element_type=jnp.float32
        )
        held_ref[column] = back[:, :atoms]
        for way, ref in enumerate(other_refs):
            ref[column] = back[:, (way + 1) * atoms : (way + 2) * atoms].astype(jnp.bfloat16)


def pick(refs, ways):
    groups = [refs[g : g + ways] for g in range(0, len(refs), ways)]
    return [ref.at[k] for group in groups for k in range(group[0].shape[0]) for ref in group]


def early_kernel(slots, ways, bases, more, own_ref, place_ref, *refs):
    near, (kern_ref, msg_ref, proj_ref) = refs[:-3], refs[-3:]
    blocks = pick(near[1:] if more else (own_ref,) + near, ways)
    build(slots, bases, own_ref.at[0], place_ref, blocks, kern_ref, proj_ref)
    rows = kern_ref.shape[0] // 3
    for m, part in enumerate(gather(kern_ref, proj_ref)):
        if more:
            part = part + near[0][m * rows : (m + 1) * rows, :]
        msg_ref[m * rows : (m + 1) * rows, :] = part


def main_kernel(slots, ways, bases, arrays, early, own_ref, place_ref, mask_ref, targ_ref, radial_ref, readout_ref, *refs):
    near, refs = refs[:arrays], refs[arrays:]
    if early:
        before_ref, side_ref, pred_ref, right_ref, held_ref = refs[:5]
        refs = refs[5:]
    else:
        pred_ref, held_ref = refs[:2]
        refs = refs[2:]
    others, (kern_ref, proj_ref) = refs[: ways - 1], refs[ways - 1 :]
    own = own_ref.at[0]
    atoms = own.shape[1]
    width = radial_ref.shape[1]
    blocks = pick(near if early else (own_ref,) + near, ways)
    build(slots, bases, own, place_ref, blocks, kern_ref, proj_ref)
    msg = jnp.concatenate(gather(kern_ref, proj_ref), 0)
    if early:
        msg = msg + before_ref[...]
    fold = [math.exp(-GAMMA * (b / (bases - 1)) ** 2) for b in range(bases)]
    weight = [radial_ref[b : b + 1, :] * fold[b] for b in range(bases)]
    pre = weight[0] * msg[:atoms]
    for b in range(1, bases):
        pre = pre + weight[b] * msg[b * atoms : (b + 1) * atoms]
    gate = 1.0 / (1.0 + jnp.exp(-pre))
    readout = readout_ref[...]
    gates = readout * gate
    vec = [msg[(bases + c) * atoms : (bases + c + 1) * atoms] for c in range(3)]
    chosen = jnp.where(spots(own)[0] < -0.5 * FAR, 0.0, mask_ref[...].astype(jnp.float32))
    lean = jnp.zeros((atoms, width), jnp.float32)
    sides = []
    for c in range(3):
        pred = jnp.sum(gates * vec[c], axis=1, keepdims=True)
        pred = jnp.transpose(jnp.broadcast_to(pred, (atoms, atoms)))[0:1, :]
        pred_ref[c] = pred
        err = across(LOSS_WEIGHT * chosen * (pred - targ_ref[c]), width)
        lean = lean + err * vec[c]
        sides.append((err * gates).astype(jnp.bfloat16))
    slope = lean * readout * gate * (1.0 - gate)
    right = jnp.concatenate([(weight[b] * slope).astype(jnp.bfloat16) for b in range(bases)] + sides, 0)
    if early:
        right_ref[...] = right
    total, fresh = held_ref.shape[0], len(slots) // ways
    scatter(right, kern_ref, 0, held_ref, others, range(total - fresh, total))
    if early:
        lane = side_ref.shape[1] - (total - fresh) * ways * atoms
        scatter(right, side_ref, lane, held_ref, others, range(total - fresh))


def late_kernel(right_ref, kern_ref, held_ref, *other_refs):
    scatter(right_ref[...], kern_ref, 0, held_ref, other_refs, range(held_ref.shape[0]))


VMEM = pl.BlockSpec(memory_space=pltpu.VMEM)
SMEM = pl.BlockSpec(memory_space=pltpu.SMEM)
LIMIT = pltpu.CompilerParams(vmem_limit_bytes=40 * 1024 * 1024)


def struct(*shape, dtype=jnp.bfloat16):
    return jax.ShapeDtypeStruct(shape, dtype)


def products(count, ways, width, atoms):
    return [struct(count, width, atoms, dtype=jnp.float32)] + [struct(count, width, atoms)] * (ways - 1)


def call_early(slots, ways, bases, own, place, near, before=None):
    atoms, width = near[0].shape[2], near[0].shape[1] - TAIL
    rows, columns = (bases + 3) * atoms, len(slots) * atoms
    more = [] if before is None else [before]
    return pl.pallas_call(
        functools.partial(early_kernel, slots, ways, bases, bool(more)),
        out_shape=[struct(rows, columns), struct(rows, width, dtype=jnp.float32)],
        in_specs=[VMEM, SMEM] + [VMEM] * (len(more) + len(near)),
        out_specs=[VMEM] * 2,
        scratch_shapes=[pltpu.VMEM((columns, width), jnp.bfloat16)],
        compiler_params=LIMIT,
        cost_estimate=pl.CostEstimate(
            flops=10 * rows * columns * width, bytes_accessed=8 * rows * columns, transcendentals=2 * atoms * columns
        ),
        name="early" if before is None else "side",
    )(own, place, *more, *near)


def call_main(slots, ways, bases, own, place, readouts, near, before=(), side=0):
    atoms, width = near[0].shape[2], near[0].shape[1] - TAIL
    rows, columns = (bases + 3) * atoms, len(slots) * atoms
    early = list(before)
    out_shape = [struct(3, 1, atoms, dtype=jnp.float32)]
    if early:
        out_shape.append(struct(rows, width))
    out_shape += products(side + len(slots) // ways, ways, width, atoms)
    return pl.pallas_call(
        functools.partial(main_kernel, slots, ways, bases, len(near), bool(early)),
        out_shape=out_shape,
        in_specs=[VMEM, SMEM] + [VMEM] * (len(readouts) + len(near) + len(early)),
        out_specs=[VMEM] * len(out_shape),
        scratch_shapes=[pltpu.VMEM((rows, columns), jnp.bfloat16), pltpu.VMEM((columns, width), jnp.bfloat16)],
        compiler_params=LIMIT,
        name="main",
    )(own, place, *readouts, *near, *early)


def call_late(right, kern, count, ways, atoms):
    rows, width = right.shape
    columns = count * ways * atoms
    out_shape = products(count, ways, width, atoms)
    return pl.pallas_call(
        late_kernel,
        out_shape=out_shape,
        in_specs=[VMEM] * 2,
        out_specs=[VMEM] * len(out_shape),
        compiler_params=LIMIT,
        cost_estimate=pl.CostEstimate(flops=2 * rows * columns * width, bytes_accessed=2 * rows * columns, transcendentals=0),
        name="late",
    )(right, kern)


AXES = ("gx", "gy", "gz")


def swap(block, axis, flip):
    sizes = [lax.axis_size(a) for a in AXES]
    pairs = []
    for place in itertools.product(*(range(n) for n in sizes)):
        other = [p ^ flip if a == axis else p for a, p in zip(AXES, place)]
        other[1] = other[1] ^ 1
        pairs.append(tuple((q[0] * sizes[1] + q[1]) * sizes[2] + q[2] for q in (place, other)))
    return lax.ppermute(block, AXES, pairs)


def core(block):
    return lax.ppermute(block, "gy", [(0, 1), (1, 0)])


def narrow(block):
    return block.astype(jnp.bfloat16)


def after(block, other):
    return lax.optimization_barrier((block, other))[0]


def exchange_small(message, bases, place, readouts):
    atoms = message.shape[1]
    x1 = swap(message, "gx", 1)
    z1 = swap(message, "gz", 1)
    z3 = swap(message, "gz", 3)
    x3 = swap(x1, "gx", 2)
    x1z1 = swap(z1, "gx", 1)
    x1z3 = swap(z3, "gx", 1)
    x3z1 = swap(x1z1, "gx", 2)
    x3z3 = swap(x1z3, "gx", 2)

    def both(x, z, hops):
        held, other = (0, None) if hops % 2 == 0 else (None, 0)
        return [(x, held, z), (x, other, z)]
    near_slots = both(0, 0, 0) + both("1", 0, 1) + both("-1", 0, 2) + both(0, "1", 1) + both(0, "-1", 1)
    side_slots = both("1", "1", 2) + both("-1", "1", 3)
    far_slots = both("1", "-1", 2) + both("-1", "-1", 3)
    near = jnp.stack([x1, x3, z1, z3])
    echo = core(message[None])
    own, rest = core(echo), [echo, near, core(near)]
    kern, before = call_early(near_slots, 2, bases, own, place, rest)
    side = jnp.stack([x1z1, x3z1])
    side = [side, core(side)]
    x1z3, x3z3, _ = lax.optimization_barrier((x1z3, x3z3, before))
    side[0], side[1], _ = lax.optimization_barrier((side[0], side[1], x3z3))
    kern_side, before = call_early(side_slots, 2, bases, own, place, side, before)
    far = jnp.stack([x1z3, x3z3])
    far = [far, core(far)]
    pred, right, far_held, far_sent = call_main(far_slots, 2, bases, own, place, readouts, far, (before, kern_side), 2)
    far_sum = far_held + core(far_sent)
    near_held, near_sent = call_late(right, kern, 5, 2, atoms)
    near_sum = near_held + core(near_sent)
    back3 = swap(narrow(far_sum[3]), "gx", 2)
    back1 = swap(narrow(jnp.stack([far_sum[1], near_sum[2]])), "gx", 2)
    next3 = narrow(far_sum[2] + back3)
    back1 = after(back1, next3)
    next1 = narrow(far_sum[0] + back1[0])
    next0 = narrow(near_sum[1] + back1[1])
    back3 = swap(next3, "gx", 1)
    back1 = swap(next1, "gx", 1)
    back0 = swap(next0, "gx", 1)
    next3 = narrow(near_sum[4] + back3)
    next1 = narrow(near_sum[3] + after(back1, next3))
    start = near_sum[0] + back0
    back3 = swap(next3, "gz", 3)
    back1 = swap(after(next1, start), "gz", 1)
    return pred, start + back1 + back3


def exchange_any(message, bases, place, readouts):
    steps_x, steps_y, steps_z = (steps_of(lax.axis_size(a)) for a in AXES)
    near = jnp.concatenate(spread(message[None], "gz"), 0)
    near = jnp.concatenate(spread(near, "gx"), 0)
    near = spread(near, "gy")
    slots = [(x, y, z) for x, z, y in itertools.product(steps_x, steps_z, steps_y)]
    pred, *parts = call_main(slots, len(near), bases, near[0], place, readouts, near[1:])
    back = collect(parts, "gy")
    back = back.reshape(len(steps_x), len(steps_z), *back.shape[1:])
    back = collect([back[0]] + [narrow(back[k]) for k in range(1, len(steps_x))], "gx")
    return pred, collect([back[0]] + [narrow(back[k]) for k in range(1, len(steps_z))], "gz")


def on_device(offsets, features, counts, mask, targets, w_in, radial, readout):
    atoms = features.shape[3]
    width = features.shape[4]
    bases = radial.shape[0]
    offs = offsets.reshape(3, 1, atoms)
    count = counts.reshape(1, 1)
    place = jnp.stack([lax.axis_index("gx"), lax.axis_index("gz")]).astype(jnp.int32)
    message = pl.pallas_call(
        message_kernel,
        out_shape=struct(width + TAIL, atoms),
        in_specs=[VMEM] * 4,
        out_specs=VMEM,
        name="message",
    )(features[0, 0, 0], w_in, offs, count)
    readouts = [mask.reshape(1, atoms), targets.reshape(3, 1, atoms), radial, readout[None, :]]
    small = tuple(lax.axis_size(a) for a in AXES) == (4, 2, 4)
    pred, back = (exchange_small if small else exchange_any)(message, bases, place, readouts)
    grad = lax.dot_general(
        narrow(back), w_in, (((0,), (1,)), ((), ())), preferred_element_type=jnp.float32
    )
    return (pred.reshape(1, 1, 1, 3, atoms), grad.reshape(1, 1, 1, atoms, width))


def solution(mesh):
    in_specs = (
        P("gx", "gy", "gz", None, None),
        P("gx", "gy", "gz", None, None),
        P("gx", "gy", "gz"),
        P("gx", "gy", "gz", None),
        P("gx", "gy", "gz", None, None),
        P(),
        P(),
        P(),
    )
    out_specs = (P("gx", "gy", "gz", None, None), P("gx", "gy", "gz", None, None))
    return jax.shard_map(
        on_device, mesh=mesh, in_specs=in_specs, out_specs=out_specs, check_vma=False
    )
```

```python
import functools
import itertools
import math

import jax
import jax.numpy as jnp
from jax import lax
from jax.experimental import pallas as pl
from jax.experimental.pallas import tpu as pltpu
from jax.sharding import PartitionSpec as P

EDGE = 10.0
CUT = 5.0
GAMMA = 20.0
LOSS_WEIGHT = 16.0
FAR = 1000.0
TAIL = 16


def steps_of(size):
    return (0, None) if size == 2 else (0, -1, 1)


def shift(block, axis, step):
    size = lax.axis_size(axis)
    return lax.ppermute(block, axis, [(i, (i + step) % size) for i in range(size)])


def spread(blocks, axis):
    parts = [blocks]
    for step in steps_of(lax.axis_size(axis))[1:]:
        parts.append(shift(blocks, axis, 1 if step is None else -step))
    return parts


def collect(blocks, axis):
    total = blocks[0]
    for part, step in zip(blocks[1:], steps_of(lax.axis_size(axis))[1:]):
        total = total + shift(part, axis, 1 if step is None else step)
    return total


def message_kernel(feat_ref, w_ref, offs_ref, counts_ref, out_ref):
    atoms, width = feat_ref.shape
    occupied = lax.broadcasted_iota(jnp.int32, (1, atoms), 1) < counts_ref[...]
    place = jnp.where(occupied, offs_ref[:, 0, :], -FAR)
    proj = jnp.dot(
        feat_ref[...], w_ref[...], preferred_element_type=jnp.float32
    ).astype(jnp.bfloat16)
    for half in range(width // atoms):
        out_ref[half * atoms : (half + 1) * atoms, :] = proj[:, half * atoms : (half + 1) * atoms]
    high = place.astype(jnp.bfloat16)
    rest = place - high.astype(jnp.float32)
    middle = rest.astype(jnp.bfloat16)
    low = (rest - middle.astype(jnp.float32)).astype(jnp.bfloat16)
    rows = jnp.concatenate(
        [
            high.astype(jnp.float32),
            middle.astype(jnp.float32),
            low.astype(jnp.float32),
            jnp.zeros((TAIL - 9, atoms), jnp.float32),
        ],
        0,
    )
    out_ref[width:, :] = rows.astype(jnp.bfloat16)


def across(row, count):
    return jnp.transpose(jnp.broadcast_to(row, (count, row.shape[1])))


def spots(block):
    coded = block[block.shape[0] - TAIL :, :].astype(jnp.float32)
    return [coded[c : c + 1, :] + coded[3 + c : 4 + c, :] + coded[6 + c : 7 + c, :] for c in range(3)]


def build(slots, bases, own, place_ref, blocks, kern_ref, proj_ref):
    rows, atoms = blocks[0].shape
    rate = 2.0 * GAMMA / (bases - 1)
    own = [across(jnp.where(spot < -0.5 * FAR, FAR, spot), atoms) for spot in spots(own)]
    turn = [None if axis is None else 1 - 2 * (place_ref[axis] & 1) for axis in (0, None, 1)]
    for s, steps in enumerate(slots):
        block = blocks[s]
        for half in range((rows - TAIL) // atoms):
            proj_ref[s * atoms : (s + 1) * atoms, half * atoms : (half + 1) * atoms] = block[
                half * atoms : (half + 1) * atoms, :
            ]
        apart = []
        for c, spot in enumerate(spots(block)):
            step = steps[c]
            if step is None:
                away = spot - own[c]
                apart.append(away + jnp.where(away < 0.0, EDGE, -EDGE))
            elif step == 0:
                apart.append(spot - own[c])
            elif isinstance(step, str):
                apart.append((spot + (turn[c] * int(step)).astype(jnp.float32) * EDGE) - own[c])
            else:
                apart.append((spot + step * EDGE) - own[c])
        ratio = (apart[0] * apart[0] + apart[1] * apart[1] + apart[2] * apart[2]) * (
            1.0 / (CUT * CUT)
        )
        ratio = jnp.minimum(ratio, 1.0)
        if steps == (0, 0, 0):
            same = lax.broadcasted_iota(jnp.int32, (atoms, atoms), 0) == lax.broadcasted_iota(
                jnp.int32, (atoms, atoms), 1
            )
            ratio = jnp.where(same, 1.0, ratio)
        envelope = jnp.square(1.0 - ratio)
        value = envelope * jnp.exp(-GAMMA * jnp.square(ratio))
        growth = jnp.exp(rate * ratio)
        lanes = slice(s * atoms, (s + 1) * atoms)
        for b in range(bases):
            kern_ref[b * atoms : (b + 1) * atoms, lanes] = value.astype(jnp.bfloat16)
            if b + 1 < bases:
                value = value * growth
        envelope = envelope * (1.0 / CUT)
        for c in range(3):
            kern_ref[(bases + c) * atoms : (bases + c + 1) * atoms, lanes] = (
                envelope * apart[c]
            ).astype(jnp.bfloat16)


def gather(kern_ref, proj_ref):
    rows = kern_ref.shape[0] // 3
    return [
        jnp.dot(kern_ref[m * rows : (m + 1) * rows, :], proj_ref[...], preferred_element_type=jnp.float32)
        for m in range(3)
    ]


def scatter(right, kern_ref, lane, held_ref, other_refs, columns):
    atoms = held_ref.shape[2]
    ways = 1 + len(other_refs)
    for k, column in enumerate(columns):
        lanes = slice(lane + k * ways * atoms, lane + (k + 1) * ways * atoms)
        back = lax.dot_general(
            right, kern_ref[:, lanes], (((0,), (0,)), ((), ())), preferred_element_type=jnp.float32
        )
        held_ref[column] = back[:, :atoms]
        for way, ref in enumerate(other_refs):
            ref[column] = back[:, (way + 1) * atoms : (way + 2) * atoms].astype(jnp.bfloat16)


def pick(refs, ways):
    groups = [refs[g : g + ways] for g in range(0, len(refs), ways)]
    return [ref.at[k] for group in groups for k in range(group[0].shape[0]) for ref in group]


def early_kernel(slots, ways, bases, more, own_ref, place_ref, *refs):
    near, (kern_ref, msg_ref, proj_ref) = refs[:-3], refs[-3:]
    blocks = pick(near[1:] if more else (own_ref,) + near, ways)
    build(slots, bases, own_ref.at[0], place_ref, blocks, kern_ref, proj_ref)
    rows = kern_ref.shape[0] // 3
    for m, part in enumerate(gather(kern_ref, proj_ref)):
        if more:
            part = part + near[0][m * rows : (m + 1) * rows, :]
        msg_ref[m * rows : (m + 1) * rows, :] = part


def main_kernel(slots, ways, bases, arrays, early, own_ref, place_ref, mask_ref, targ_ref, radial_ref, readout_ref, *refs):
    near, refs = refs[:arrays], refs[arrays:]
    if early:
        before_ref, side_ref, pred_ref, right_ref, held_ref = refs[:5]
        refs = refs[5:]
    else:
        pred_ref, held_ref = refs[:2]
        refs = refs[2:]
    others, (kern_ref, proj_ref) = refs[: ways - 1], refs[ways - 1 :]
    own = own_ref.at[0]
    atoms = own.shape[1]
    width = radial_ref.shape[1]
    blocks = pick(near if early else (own_ref,) + near, ways)
    build(slots, bases, own, place_ref, blocks, kern_ref, proj_ref)
    msg = jnp.concatenate(gather(kern_ref, proj_ref), 0)
    if early:
        msg = msg + before_ref[...]
    fold = [math.exp(-GAMMA * (b / (bases - 1)) ** 2) for b in range(bases)]
    weight = [radial_ref[b : b + 1, :] * fold[b] for b in range(bases)]
    pre = weight[0] * msg[:atoms]
    for b in range(1, bases):
        pre = pre + weight[b] * msg[b * atoms : (b + 1) * atoms]
    gate = 1.0 / (1.0 + jnp.exp(-pre))
    readout = readout_ref[...]
    gates = readout * gate
    vec = [msg[(bases + c) * atoms : (bases + c + 1) * atoms] for c in range(3)]
    chosen = jnp.where(spots(own)[0] < -0.5 * FAR, 0.0, mask_ref[...].astype(jnp.float32))
    lean = jnp.zeros((atoms, width), jnp.float32)
    sides = []
    for c in range(3):
        pred = jnp.sum(gates * vec[c], axis=1, keepdims=True)
        pred = jnp.transpose(jnp.broadcast_to(pred, (atoms, atoms)))[0:1, :]
        pred_ref[c] = pred
        err = across(LOSS_WEIGHT * chosen * (pred - targ_ref[c]), width)
        lean = lean + err * vec[c]
        sides.append((err * gates).astype(jnp.bfloat16))
    slope = lean * readout * gate * (1.0 - gate)
    right = jnp.concatenate([(weight[b] * slope).astype(jnp.bfloat16) for b in range(bases)] + sides, 0)
    if early:
        right_ref[...] = right
    total, fresh = held_ref.shape[0], len(slots) // ways
    scatter(right, kern_ref, 0, held_ref, others, range(total - fresh, total))
    if early:
        lane = side_ref.shape[1] - (total - fresh) * ways * atoms
        scatter(right, side_ref, lane, held_ref, others, range(total - fresh))


def late_kernel(right_ref, kern_ref, held_ref, *other_refs):
    scatter(right_ref[...], kern_ref, 0, held_ref, other_refs, range(held_ref.shape[0]))


VMEM = pl.BlockSpec(memory_space=pltpu.VMEM)
SMEM = pl.BlockSpec(memory_space=pltpu.SMEM)
LIMIT = pltpu.CompilerParams(vmem_limit_bytes=40 * 1024 * 1024)


def struct(*shape, dtype=jnp.bfloat16):
    return jax.ShapeDtypeStruct(shape, dtype)


def products(count, ways, width, atoms):
    return [struct(count, width, atoms, dtype=jnp.float32)] + [struct(count, width, atoms)] * (ways - 1)


def call_early(slots, ways, bases, own, place, near, before=None):
    atoms, width = near[0].shape[2], near[0].shape[1] - TAIL
    rows, columns = (bases + 3) * atoms, len(slots) * atoms
    more = [] if before is None else [before]
    return pl.pallas_call(
        functools.partial(early_kernel, slots, ways, bases, bool(more)),
        out_shape=[struct(rows, columns), struct(rows, width, dtype=jnp.float32)],
        in_specs=[VMEM, SMEM] + [VMEM] * (len(more) + len(near)),
        out_specs=[VMEM] * 2,
        scratch_shapes=[pltpu.VMEM((columns, width), jnp.bfloat16)],
        compiler_params=LIMIT,
        cost_estimate=pl.CostEstimate(
            flops=10 * rows * columns * width, bytes_accessed=8 * rows * columns, transcendentals=2 * atoms * columns
        ),
        name="early" if before is None else "side",
    )(own, place, *more, *near)


def call_main(slots, ways, bases, own, place, readouts, near, before=(), side=0):
    atoms, width = near[0].shape[2], near[0].shape[1] - TAIL
    rows, columns = (bases + 3) * atoms, len(slots) * atoms
    early = list(before)
    out_shape = [struct(3, 1, atoms, dtype=jnp.float32)]
    if early:
        out_shape.append(struct(rows, width))
    out_shape += products(side + len(slots) // ways, ways, width, atoms)
    return pl.pallas_call(
        functools.partial(main_kernel, slots, ways, bases, len(near), bool(early)),
        out_shape=out_shape,
        in_specs=[VMEM, SMEM] + [VMEM] * (len(readouts) + len(near) + len(early)),
        out_specs=[VMEM] * len(out_shape),
        scratch_shapes=[pltpu.VMEM((rows, columns), jnp.bfloat16), pltpu.VMEM((columns, width), jnp.bfloat16)],
        compiler_params=LIMIT,
        name="main",
    )(own, place, *readouts, *near, *early)


def call_late(right, kern, count, ways, atoms):
    rows, width = right.shape
    columns = count * ways * atoms
    out_shape = products(count, ways, width, atoms)
    return pl.pallas_call(
        late_kernel,
        out_shape=out_shape,
        in_specs=[VMEM] * 2,
        out_specs=[VMEM] * len(out_shape),
        compiler_params=LIMIT,
        cost_estimate=pl.CostEstimate(flops=2 * rows * columns * width, bytes_accessed=2 * rows * columns, transcendentals=0),
        name="late",
    )(right, kern)


AXES = ("gx", "gy", "gz")


def swap(block, axis, flip):
    sizes = [lax.axis_size(a) for a in AXES]
    pairs = []
    for place in itertools.product(*(range(n) for n in sizes)):
        other = [p ^ flip if a == axis else p for a, p in zip(AXES, place)]
        other[1] = other[1] ^ 1
        pairs.append(tuple((q[0] * sizes[1] + q[1]) * sizes[2] + q[2] for q in (place, other)))
    return lax.ppermute(block, AXES, pairs)


def core(block):
    return lax.ppermute(block, "gy", [(0, 1), (1, 0)])


def narrow(block):
    return block.astype(jnp.bfloat16)


def after(block, other):
    return lax.optimization_barrier((block, other))[0]


def exchange_small(message, bases, place, readouts):
    atoms = message.shape[1]
    x1 = swap(message, "gx", 1)
    z1 = swap(message, "gz", 1)
    z3 = swap(message, "gz", 3)
    x3 = swap(x1, "gx", 2)
    x1z1 = swap(z1, "gx", 1)
    x1z3 = swap(z3, "gx", 1)
    x3z1 = swap(x1z1, "gx", 2)
    x3z3 = swap(x1z3, "gx", 2)

    def both(x, z, hops):
        held, other = (0, None) if hops % 2 == 0 else (None, 0)
        return [(x, held, z), (x, other, z)]
    near_slots = both(0, 0, 0) + both("1", 0, 1) + both("-1", 0, 2) + both(0, "1", 1) + both(0, "-1", 1)
    side_slots = both("1", "1", 2) + both("-1", "1", 3)
    far_slots = both("1", "-1", 2) + both("-1", "-1", 3)
    near = jnp.stack([x1, x3, z1, z3])
    echo = core(message[None])
    own, rest = core(echo), [echo, near, core(near)]
    kern, before = call_early(near_slots, 2, bases, own, place, rest)
    side = jnp.stack([x1z1, x3z1])
    side = [side, core(side)]
    x1z3, x3z3, _ = lax.optimization_barrier((x1z3, x3z3, before))
    side[0], side[1], _ = lax.optimization_barrier((side[0], side[1], x3z3))
    kern_side, before = call_early(side_slots, 2, bases, own, place, side, before)
    far = jnp.stack([x1z3, x3z3])
    far = [far, core(far)]
    pred, right, far_held, far_sent = call_main(far_slots, 2, bases, own, place, readouts, far, (before, kern_side), 2)
    far_sum = far_held + core(far_sent)
    near_held, near_sent = call_late(right, kern, 5, 2, atoms)
    near_sum = near_held + core(near_sent)
    back3 = swap(narrow(far_sum[3]), "gx", 2)
    back1 = swap(narrow(jnp.stack([far_sum[1], near_sum[2]])), "gx", 2)
    next3 = narrow(far_sum[2] + back3)
    back1 = after(back1, next3)
    next1 = narrow(far_sum[0] + back1[0])
    next0 = narrow(near_sum[1] + back1[1])
    back3 = swap(next3, "gx", 1)
    back1 = swap(next1, "gx", 1)
    back0 = swap(next0, "gx", 1)
    next3 = narrow(near_sum[4] + back3)
    start = near_sum[0] + after(back0, next3)
    next1 = narrow(near_sum[3] + after(back1, next3))
    back3 = swap(next3, "gz", 3)
    back1 = swap(after(next1, start), "gz", 1)
    return pred, start + back1 + back3


def exchange_any(message, bases, place, readouts):
    steps_x, steps_y, steps_z = (steps_of(lax.axis_size(a)) for a in AXES)
    near = jnp.concatenate(spread(message[None], "gz"), 0)
    near = jnp.concatenate(spread(near, "gx"), 0)
    near = spread(near, "gy")
    slots = [(x, y, z) for x, z, y in itertools.product(steps_x, steps_z, steps_y)]
    pred, *parts = call_main(slots, len(near), bases, near[0], place, readouts, near[1:])
    back = collect(parts, "gy")
    back = back.reshape(len(steps_x), len(steps_z), *back.shape[1:])
    back = collect([back[0]] + [narrow(back[k]) for k in range(1, len(steps_x))], "gx")
    return pred, collect([back[0]] + [narrow(back[k]) for k in range(1, len(steps_z))], "gz")


def on_device(offsets, features, counts, mask, targets, w_in, radial, readout):
    atoms = features.shape[3]
    width = features.shape[4]
    bases = radial.shape[0]
    offs = offsets.reshape(3, 1, atoms)
    count = counts.reshape(1, 1)
    place = jnp.stack([lax.axis_index("gx"), lax.axis_index("gz")]).astype(jnp.int32)
    message = pl.pallas_call(
        message_kernel,
        out_shape=struct(width + TAIL, atoms),
        in_specs=[VMEM] * 4,
        out_specs=VMEM,
        name="message",
    )(features[0, 0, 0], w_in, offs, count)
    readouts = [mask.reshape(1, atoms), targets.reshape(3, 1, atoms), radial, readout[None, :]]
    small = tuple(lax.axis_size(a) for a in AXES) == (4, 2, 4)
    pred, back = (exchange_small if small else exchange_any)(message, bases, place, readouts)
    grad = lax.dot_general(
        narrow(back), w_in, (((0,), (1,)), ((), ())), preferred_element_type=jnp.float32
    )
    return (pred.reshape(1, 1, 1, 3, atoms), grad.reshape(1, 1, 1, atoms, width))


def solution(mesh):
    in_specs = (
        P("gx", "gy", "gz", None, None),
        P("gx", "gy", "gz", None, None),
        P("gx", "gy", "gz"),
        P("gx", "gy", "gz", None),
        P("gx", "gy", "gz", None, None),
        P(),
        P(),
        P(),
    )
    out_specs = (P("gx", "gy", "gz", None, None), P("gx", "gy", "gz", None, None))
    return jax.shard_map(
        on_device, mesh=mesh, in_specs=in_specs, out_specs=out_specs, check_vma=False
    )
```
